512 devices in a mesh: band: 16 (over z), fft: 16 (over x, y), pool: 2 (over core).
Axes of the slice: x: 4, y: 4, z: 16, core: 2. Of those that a mesh axis runs over, the one named last changes fastest.
Arguments:
- orbitals: float32 [32, 64, 4096], P('band', 'fft'), may hold values from -5 to 5
- kernel: float32 [64, 4096], P(None, 'fft'), may hold values from 0.05 to 2, as said below
Outputs:
- exchange_field: float32 [32, 64, 4096], P('band', 'fft')
The draws below stay inside these ranges and needn't reach their ends.
Inputs may be any that keep to these rules, and one draw needn't show every extreme that they name: kernel is even: its value at (kx, ky, kz) equals its value at ((64 - kx) % 64, (64 - ky) % 64, (64 - kz) % 64), with 64, 64, 64 the grid sizes.
All inputs are finite; a program needn't handle non-finite values.
Results may differ from the reference program's by a relative error of at most 0.000054.
Values sent between devices are 32-bit elements; how exact they have to be, the bound alone decides.
No kernel may reach another device: no remote copies, remote signals or barrier semaphores. Data moves between devices by JAX's collectives and lax.ppermute only.
A program may use at most 64 MiB of HBM per device.

```python
import math
import jax
import jax.numpy as jnp
from jax import lax

NX = 64
NY = 64
NZ = 64
BANDS = 32


def draw_kernel(key, part):
    key = jax.random.fold_in(key, 7)
    base = jnp.exp(jax.random.uniform(key, (NX, NY, NZ), jnp.float32, math.log(0.05), math.log(2.0)))
    mirrored = jnp.roll(jnp.flip(base, (0, 1, 2)), 1, axis=(0, 1, 2))
    return (0.5 * (base + mirrored)).reshape(NX, NY * NZ)


def level_of(rng, dims, cuts, least, largest):
    factor_of, own = 1.0, jax.random.fold_in(rng, 6)
    for axis_at, blocks in cuts:
        steps = jnp.exp(jax.random.uniform(jax.random.fold_in(own, axis_at), (blocks,), jnp.float32, least / len(cuts), largest / len(cuts)))
        factor_of = factor_of * jnp.repeat(steps, dims[axis_at] // blocks).reshape([-1 if axis == axis_at else 1 for axis in range(len(dims))])
    return factor_of


def centred(own_key, dims, deviation, limit, cuts=(), kind=jnp.bfloat16):
    factor_of = level_of(own_key, dims, cuts, -0.22, 0.18) if cuts else 1.0
    entries = jax.random.normal(own_key, dims, jnp.float32) * deviation * factor_of
    return jnp.minimum(jnp.maximum(entries, -limit), limit).astype(kind)


def setup_inputs(seed: int = 0) -> dict:
    key_list = jax.random.split(jax.random.key(seed), 3)
    orbitals = centred(key_list[0], (BANDS, NX, NY * NZ), 0.7, 5.0, ((0, 16), (1, 16)), jnp.float32)
    kernel = draw_kernel(jax.random.fold_in(key_list[2], 71), 0)
    return dict(orbitals=orbitals, kernel=kernel)


def reference(orbitals, kernel):
    orbital_grid = orbitals.reshape(BANDS, NX, NY, NZ)
    coulomb = kernel.reshape(NX, NY, NZ)

    def exchange_of(target):
        density = target[None] * orbital_grid
        spectrum = jnp.fft.fftn(density, axes=(1, 2, 3))
        potential = jnp.real(jnp.fft.ifftn(coulomb[None] * spectrum, axes=(1, 2, 3)))
        return -jnp.sum(potential * orbital_grid, axis=0)

    field = lax.map(exchange_of, orbital_grid)
    return field.reshape(BANDS, NX, NY * NZ).astype(jnp.float32)
```

```python
import functools

import jax
import jax.numpy as jnp
import ml_dtypes
import numpy as np
from jax import lax
from jax.experimental import pallas as pl
from jax.experimental.pallas import tpu as pltpu
from jax.sharding import PartitionSpec as P

N = 64
CELLS = N * N * N
LANES = 2 * N
PEERS = 32
UNITS = 9
ROWS = 8 * UNITS

OFFSETS = (0, 2, -3, -4, 4)
MEETINGS = ((3, 2), (0, 1), (2, 0), (3, 0), (2, 1), (3, 1), (2, 4))
OPPOSITE = (3, 4)


def wave_parts(rows, columns):
    angle = 2.0 * np.pi / N * ((rows * columns) % N)
    return np.cos(angle), np.sin(angle)


def split_table(table):
    high = table.astype(ml_dtypes.bfloat16)
    low = (table - high.astype(np.float64)).astype(ml_dtypes.bfloat16)
    return np.stack([high, low])


def tables():
    index = np.arange(N)
    cosine, sine = wave_parts(index[:, None], index[None, :])
    turn = np.stack([np.stack([cosine, sine]), np.stack([-sine, cosine])])
    two = np.eye(2)
    along_z = np.einsum("oikz,ab->iazobk", turn, two).reshape(256, 256)
    along_y = np.einsum("oiky,ab->kaoiby", turn, two)
    along_y = along_y.reshape(32, 2, 2, 2, 2, 2, N).transpose(0, 2, 3, 1, 5, 4, 6)
    along_y = along_y.reshape(256, 256)
    along_x = np.einsum("oikx,ab->koaxib", turn, two).reshape(256, 256)
    return [split_table(t) for t in (along_z, along_y, along_x, along_x.T, along_y.T, along_z.T)]


def halves(value):
    high = value.astype(jnp.bfloat16)
    low = (value - high.astype(jnp.float32)).astype(jnp.bfloat16)
    return high, low


def dot(left, right):
    return jnp.dot(left, right, preferred_element_type=jnp.float32)


def times_table(value, table):
    high, low = halves(value)
    return dot(high, table[0]) + dot(low, table[0]) + dot(high, table[1])


def table_times(table, value):
    high, low = halves(value)
    return dot(table[0], high) + dot(table[0], low) + dot(table[1], high)


def swap(value):
    return pltpu.roll(value, N, 1)


def forward_kernel(side, b0, b1, b2, b3, b4, table_z, table_y, out):
    blocks = (b0, b1, b2, b3, b4)

    def unit(number, plane):
        if number < 14:
            left, right = MEETINGS[number // 2]
            right = blocks[right][plane]
            return blocks[left][plane] * (swap(right) if number % 2 else right)
        own = b0[plane]
        if number == 14:
            return own * own
        if number == 15:
            return own * swap(own)
        if number == 16:
            right = blocks[OPPOSITE[1]][plane]
            return blocks[OPPOSITE[0]][plane] * jnp.where(side[0] == 0, right, swap(right))
        return jnp.zeros((N, LANES), jnp.float32)

    for u in range(UNITS):
        density = jnp.concatenate(
            [
                jnp.concatenate([unit(2 * u, plane), unit(2 * u + 1, plane)], axis=1)
                for plane in range(2)
            ],
            axis=0,
        )
        rows = times_table(density, table_z)
        rows = jnp.concatenate(
            [
                rows[plane * N : plane * N + N, part * LANES : part * LANES + LANES]
                for plane in range(2)
                for part in range(2)
            ],
            axis=0,
        )
        out[:, 8 * u : 8 * u + 8, :] = table_times(table_y, rows).reshape(PEERS, 8, LANES)


def middle_kernel(spectra, coulomb, table_x, table_x_back, out):
    for u in range(UNITS):
        rows = spectra[:, 8 * u : 8 * u + 8, :].reshape(256, LANES)
        rows = table_times(table_x, rows) * coulomb[...]
        out[:, 8 * u : 8 * u + 8, :] = table_times(table_x_back, rows).reshape(PEERS, 8, LANES)


def backward_kernel(
    side, returned, b0, b1, b2, b3, b4, table_y_back, table_z_back, f0, f1, f2, f3, f4
):
    blocks = (b0, b1, b2, b3, b4)
    fields = (f0, f1, f2, f3, f4)
    started = set()

    def add(place, plane, value):
        if (place, plane) in started:
            fields[place][plane] += value
        else:
            started.add((place, plane))
            fields[place][plane] = value

    def collect(number, plane, potential):
        if number < 14:
            left, right = MEETINGS[number // 2]
            if number % 2:
                add(left, plane, potential * swap(blocks[right][plane]))
                add(right, plane, swap(potential * blocks[left][plane]))
            else:
                add(left, plane, potential * blocks[right][plane])
                add(right, plane, potential * blocks[left][plane])
        elif number == 14:
            add(0, plane, potential * b0[plane])
        elif number == 15:
            add(0, plane, potential * swap(b0[plane]))
        elif number == 16:
            left, right = OPPOSITE
            partner = blocks[right][plane]
            add(left, plane, potential * jnp.where(side[0] == 0, partner, swap(partner)))
            given = potential * blocks[left][plane]
            add(right, plane, jnp.where(side[0] == 0, given, swap(given)))

    for u in range(UNITS):
        rows = returned[:, 8 * u : 8 * u + 8, :].reshape(256, LANES)
        rows = table_times(table_y_back, rows)
        rows = jnp.concatenate(
            [
                jnp.concatenate(
                    [
                        rows[plane * LANES + part * N : plane * LANES + part * N + N]
                        for part in range(2)
                    ],
                    axis=1,
                )
                for plane in range(2)
            ],
            axis=0,
        )
        rows = times_table(rows, table_z_back)
        for plane in range(2):
            for half in range(2):
                collect(
                    2 * u + half,
                    plane,
                    rows[plane * N : plane * N + N, half * LANES : half * LANES + LANES],
                )


VMEM = pl.BlockSpec(memory_space=pltpu.VMEM)
SMEM = pl.BlockSpec(memory_space=pltpu.SMEM)
PARAMS = pltpu.CompilerParams(vmem_limit_bytes=32 * 1024 * 1024)
CHUNKS = jax.ShapeDtypeStruct((PEERS, ROWS, LANES), jnp.float32)
BLOCK = jax.ShapeDtypeStruct((2, N, LANES), jnp.float32)


def forward(side, blocks, table_z, table_y):
    return pl.pallas_call(
        forward_kernel,
        out_shape=CHUNKS,
        in_specs=[SMEM] + [VMEM] * 7,
        out_specs=VMEM,
        compiler_params=PARAMS,
    )(side, *blocks, table_z, table_y)


def middle(spectra, coulomb, table_x, table_x_back):
    return pl.pallas_call(
        middle_kernel,
        out_shape=CHUNKS,
        in_specs=[VMEM] * 4,
        out_specs=VMEM,
        compiler_params=PARAMS,
    )(spectra, coulomb, table_x, table_x_back)


def backward(side, returned, blocks, table_y_back, table_z_back):
    return pl.pallas_call(
        backward_kernel,
        out_shape=[BLOCK] * 5,
        in_specs=[SMEM] + [VMEM] * 8,
        out_specs=[VMEM] * 5,
        compiler_params=PARAMS,
    )(side, returned, *blocks, table_y_back, table_z_back)


def along_band(value, steps):
    count = lax.axis_size("band")
    pairs = [(source, (source + steps) % count) for source in range(count)]
    return lax.ppermute(value, "band", pairs)


def spread_kernel(kernel, pool_at):
    mine = lax.dynamic_slice_in_dim(kernel, pool_at * LANES, LANES, 1)
    mine = mine.reshape(N, 1, 2, 1, N) * (-1.0 / CELLS)
    return jnp.broadcast_to(mine, (N, 2, 2, 2, N)).reshape(256, LANES)


def exchange(value):
    return lax.all_to_all(value, ("fft", "pool"), split_axis=0, concat_axis=0, tiled=True)


def local(orbitals, kernel):
    pool_at = lax.axis_index("pool")
    side = (lax.axis_index("band") // 8).astype(jnp.int32).reshape(1)
    table_z, table_y, table_x, table_x_back, table_y_back, table_z_back = [
        jnp.asarray(t) for t in tables()
    ]
    own = lax.dynamic_slice_in_dim(orbitals, 2 * pool_at, 2, 1)
    own = own.reshape(2, 2, N, N).transpose(1, 2, 0, 3).reshape(2, N, LANES)
    blocks = [along_band(own, -s) if s else own for s in OFFSETS]
    coulomb = spread_kernel(kernel, pool_at)
    spectra = exchange(forward(side, blocks, table_z, table_y))
    returned = exchange(middle(spectra, coulomb, table_x, table_x_back))
    fields = backward(side, returned, blocks, table_y_back, table_z_back)
    total = functools.reduce(
        jnp.add, [along_band(f, s) if s else f for s, f in zip(OFFSETS, fields)]
    )
    both = lax.all_gather(total, "pool", tiled=True)
    return both.reshape(4, N, 2, N).transpose(2, 0, 1, 3).reshape(2, 4, N * N)


def solution(mesh):
    return jax.shard_map(
        local,
        mesh=mesh,
        in_specs=(P("band", "fft", None), P(None, "fft")),
        out_specs=P("band", "fft", None),
        check_vma=False,
    )
```

```python
import jax
import jax.numpy as jnp
import ml_dtypes
import numpy as np
from jax import lax
from jax.experimental import pallas as pl
from jax.experimental.pallas import tpu as pltpu
from jax.sharding import PartitionSpec as P

N = 64
CELLS = N * N * N
LANES = 2 * N
PEERS = 32
UNITS = 9
ROWS = 8 * UNITS

NEAR = (2, -3)
FAR = (4, -4)
MEETINGS = ((4, 2), (0, 1), (2, 0), (4, 0), (2, 1), (4, 1), (2, 3))
OPPOSITE = (4, 3)


def wave_parts(rows, columns):
    angle = 2.0 * np.pi / N * ((rows * columns) % N)
    return np.cos(angle), np.sin(angle)


def split_table(table):
    high = table.astype(ml_dtypes.bfloat16)
    low = (table - high.astype(np.float64)).astype(ml_dtypes.bfloat16)
    return np.stack([high, low])


def tables():
    index = np.arange(N)
    cosine, sine = wave_parts(index[:, None], index[None, :])
    turn = np.stack([np.stack([cosine, sine]), np.stack([-sine, cosine])])
    two = np.eye(2)
    along_z = np.einsum("oikz,ab->iazobk", turn, two).reshape(256, 256)
    along_y = np.einsum("oiky,ab->kaoiby", turn, two)
    along_y = along_y.reshape(32, 2, 2, 2, 2, 2, N).transpose(0, 2, 3, 1, 5, 4, 6)
    along_y = along_y.reshape(256, 256)
    along_x = np.einsum("oikx,ab->oakxib", turn, two).reshape(256, 256)
    return [split_table(t) for t in (along_z, along_y, along_x, along_x.T, along_y.T, along_z.T)]


def halves(value):
    high = value.astype(jnp.bfloat16)
    low = (value - high.astype(jnp.float32)).astype(jnp.bfloat16)
    return high, low


def dot(left, right):
    return jnp.dot(left, right, preferred_element_type=jnp.float32)


def times_table(value, table):
    high, low = halves(value)
    return dot(high, table[0]) + dot(low, table[0]) + dot(high, table[1])


def table_times(table, value):
    high, low = halves(value)
    return dot(table[0], high) + dot(table[0], low) + dot(table[1], high)


def swap(value):
    return pltpu.roll(value, N, 1)


def block_reader(own, near, far):
    half = 2 * lax.axis_index("pool")

    def read(place, plane):
        if place == 0:
            return own[half + plane]
        return (near, far)[(place - 1) // 2][(place - 1) % 2 * 4 + half + plane]

    return read


def first_side():
    return lax.axis_index("band") < 8


def forward_kernel(own, near, far, table_z_far, table_y_far, out, table_z, table_y, arrived):
    copies = [
        pltpu.make_async_copy(source, target, arrived.at[at])
        for at, (source, target) in enumerate(((table_z_far, table_z), (table_y_far, table_y)))
    ]
    for copy in copies:
        copy.start()
    read = block_reader(own, near, far)

    def unit(number, plane):
        if number < 14:
            left, right = MEETINGS[number // 2]
            right = read(right, plane)
            return read(left, plane) * (swap(right) if number % 2 else right)
        if number == 14:
            return read(0, plane) * read(0, plane)
        if number == 15:
            return read(0, plane) * swap(read(0, plane))
        if number == 16:
            left, right = OPPOSITE
            right = read(right, plane)
            return read(left, plane) * jnp.where(first_side(), right, swap(right))
        return jnp.zeros((N, LANES), jnp.float32)

    for copy in copies:
        copy.wait()
    for u in range(UNITS):
        density = jnp.concatenate(
            [
                jnp.concatenate([unit(2 * u, plane), unit(2 * u + 1, plane)], axis=1)
                for plane in range(2)
            ],
            axis=0,
        )
        rows = times_table(density, table_z)
        rows = jnp.concatenate(
            [
                rows[plane * N : plane * N + N, part * LANES : part * LANES + LANES]
                for plane in range(2)
                for part in range(2)
            ],
            axis=0,
        )
        out[:, 8 * u : 8 * u + 8, :] = table_times(table_y, rows).reshape(PEERS, 8, LANES)


def middle_kernel(spectra, kernel, table_x, table_x_back, out):
    at = pl.multiple_of(lax.axis_index("pool") * LANES, LANES)
    mine = kernel[:, pl.ds(at, LANES)] * (-1.0 / CELLS)
    turned = swap(mine)
    low = lax.broadcasted_iota(jnp.int32, (N, LANES), 1) < N
    even, odd = jnp.where(low, mine, turned), jnp.where(low, turned, mine)
    coulomb = jnp.concatenate([even, odd, even, odd], axis=0)
    for u in range(UNITS):
        rows = spectra[:, 8 * u : 8 * u + 8, :].reshape(256, LANES)
        rows = table_times(table_x, rows) * coulomb
        out[:, 8 * u : 8 * u + 8, :] = table_times(table_x_back, rows).reshape(PEERS, 8, LANES)


def backward_kernel(
    returned, own, near, far, table_y_back, table_z_back, own_field, near_fields, far_fields
):
    read = block_reader(own, near, far)
    started = set()

    def add(place, plane, value):
        if place == 0:
            field, at = own_field, (plane,)
        else:
            field, at = (near_fields, far_fields)[(place - 1) // 2], ((place - 1) % 2, plane)
        if (place, plane) in started:
            field[at] += value
        else:
            started.add((place, plane))
            field[at] = value

    def collect(number, plane, potential):
        if number < 14:
            left, right = MEETINGS[number // 2]
            if number % 2:
                add(left, plane, potential * swap(read(right, plane)))
                add(right, plane, swap(potential * read(left, plane)))
            else:
                add(left, plane, potential * read(right, plane))
                add(right, plane, potential * read(left, plane))
        elif number == 14:
            add(0, plane, potential * read(0, plane))
        elif number == 15:
            add(0, plane, potential * swap(read(0, plane)))
        elif number == 16:
            left, right = OPPOSITE
            partner = read(right, plane)
            add(left, plane, potential * jnp.where(first_side(), partner, swap(partner)))
            given = potential * read(left, plane)
            add(right, plane, jnp.where(first_side(), given, swap(given)))

    for u in range(UNITS):
        rows = returned[:, 8 * u : 8 * u + 8, :].reshape(256, LANES)
        rows = table_times(table_y_back, rows)
        rows = jnp.concatenate(
            [
                jnp.concatenate(
                    [
                        rows[plane * LANES + part * N : plane * LANES + part * N + N]
                        for part in range(2)
                    ],
                    axis=1,
                )
                for plane in range(2)
            ],
            axis=0,
        )
        rows = times_table(rows, table_z_back)
        for plane in range(2):
            for half in range(2):
                collect(
                    2 * u + half,
                    plane,
                    rows[plane * N : plane * N + N, half * LANES : half * LANES + LANES],
                )


VMEM = pl.BlockSpec(memory_space=pltpu.VMEM)
ANY = pl.BlockSpec(memory_space=pl.ANY)
PARAMS = pltpu.CompilerParams(vmem_limit_bytes=32 * 1024 * 1024)
CHUNKS = jax.ShapeDtypeStruct((PEERS, ROWS, LANES), jnp.float32)
FIELD = jax.ShapeDtypeStruct((2, N, LANES), jnp.float32)
FIELDS = jax.ShapeDtypeStruct((2, 2, N, LANES), jnp.float32)
TABLE = pltpu.VMEM((2, 256, 256), jnp.bfloat16)


def forward(own, near, far, table_z, table_y):
    return pl.pallas_call(
        forward_kernel,
        out_shape=CHUNKS,
        in_specs=[VMEM] * 3 + [ANY] * 2,
        out_specs=VMEM,
        scratch_shapes=[TABLE, TABLE, pltpu.SemaphoreType.DMA((2,))],
        compiler_params=PARAMS,
    )(own, near, far, table_z, table_y)


def middle(spectra, kernel, table_x, table_x_back):
    return pl.pallas_call(
        middle_kernel,
        out_shape=CHUNKS,
        in_specs=[VMEM] * 4,
        out_specs=VMEM,
        compiler_params=PARAMS,
    )(spectra, kernel, table_x, table_x_back)


def backward(returned, own, near, far, table_y_back, table_z_back):
    return pl.pallas_call(
        backward_kernel,
        out_shape=[FIELD, FIELDS, FIELDS],
        in_specs=[VMEM] * 6,
        out_specs=[VMEM] * 3,
        compiler_params=PARAMS,
    )(returned, own, near, far, table_y_back, table_z_back)


def along_band(value, steps):
    count = lax.axis_size("band")
    pairs = [
        (2 * source + core, 2 * ((source + steps[core]) % count) + core)
        for source in range(count)
        for core in range(2)
    ]
    return lax.ppermute(value, ("band", "pool"), pairs)


def both_cores(value):
    return lax.all_gather(value, "pool", tiled=True)


def exchange(value):
    return lax.all_to_all(value, ("fft", "pool"), split_axis=0, concat_axis=0, tiled=True)


def send_home(fields, steps, pool_at):
    halves_of = both_cores(fields).reshape(2, 2, 2, N, LANES)
    mine = lax.dynamic_index_in_dim(halves_of, pool_at, 1, keepdims=False)
    return along_band(mine.reshape(4, N, LANES), steps)


def local(orbitals, kernel):
    pool_at = lax.axis_index("pool")
    table_z, table_y, table_x, table_x_back, table_y_back, table_z_back = [
        jnp.asarray(t) for t in tables()
    ]
    own = orbitals.reshape(2, 4, N, N).transpose(1, 2, 0, 3).reshape(4, N, LANES)
    near = both_cores(along_band(own, [-s for s in NEAR]))
    far = both_cores(along_band(own, [-s for s in FAR]))
    spectra = exchange(forward(own, near, far, table_z, table_y))
    returned = exchange(middle(spectra, kernel, table_x, table_x_back))
    own_field, near_fields, far_fields = backward(
        returned, own, near, far, table_y_back, table_z_back
    )
    total = send_home(near_fields, NEAR, pool_at) + send_home(far_fields, FAR, pool_at)
    placed = jnp.where(
        (jnp.arange(2) == pool_at).reshape(2, 1, 1, 1), own_field[None], 0.0
    ).reshape(4, N, LANES)
    both = both_cores(total + placed).reshape(2, 4, N, LANES)
    field = both[0] + both[1]
    return field.reshape(4, N, 2, N).transpose(2, 0, 1, 3).reshape(2, 4, N * N)


def solution(mesh):
    return jax.shard_map(
        local,
        mesh=mesh,
        in_specs=(P("band", "fft", None), P(None, "fft")),
        out_specs=P("band", "fft", None),
        check_vma=False,
    )
```

```python
import jax
import jax.numpy as jnp
import ml_dtypes
import numpy as np
from jax import lax
from jax.experimental import pallas as pl
from jax.experimental.pallas import tpu as pltpu
from jax.sharding import PartitionSpec as P

N = 64
HALF = N // 2
CELLS = N * N * N
LANES = 2 * N
PEERS = 16
UNITS = 4
ROWS = 32 * UNITS + 16

NEAR = (2, -3)
FAR = (4, -4)
MEETINGS = (((0, 1), (0, 2)), ((1, 4), (2, 3)), ((2, 4), (0, 4)), ((1, 2), None))
SQUARES = (0, 0)
OPPOSITE = (4, 3)


def wave_parts(rows, columns):
    angle = 2.0 * np.pi / N * ((rows * columns) % N)
    return np.cos(angle), np.sin(angle)


def split_table(table):
    high = table.astype(ml_dtypes.bfloat16)
    low = (table - high.astype(np.float64)).astype(ml_dtypes.bfloat16)
    return np.stack([high, low])


def tables():
    index = np.arange(N)
    cosine, sine = wave_parts(index[:, None], index[None, :])
    turn = np.stack([np.stack([cosine, sine]), np.stack([-sine, cosine])])
    two = np.eye(2)
    along_z = np.einsum("oikz,ab->iazobk", turn, two).reshape(256, 256)
    along_y = np.einsum("oiky,ab->kaoiby", turn, two)
    along_y = along_y.reshape(PEERS, 2, 2, 2, 2, 2, 2, HALF, 2)
    along_y = along_y.transpose(0, 1, 3, 4, 2, 6, 5, 8, 7).reshape(256, 256)
    along_x = np.einsum("oikx,ab->oakxib", turn, two).reshape(256, 256)
    return [split_table(t) for t in (along_z, along_y, along_x, along_x.T, along_y.T, along_z.T)]


def halves(value):
    high = value.astype(jnp.bfloat16)
    low = (value - high.astype(jnp.float32)).astype(jnp.bfloat16)
    return high, low


def dot(left, right):
    return jnp.dot(left, right, preferred_element_type=jnp.float32)


def times_table(value, table):
    high, low = halves(value)
    return dot(high, table[0]) + dot(low, table[0]) + dot(high, table[1])


def table_times(table, value):
    high, low = halves(value)
    return dot(table[0], high) + dot(table[0], low) + dot(table[1], high)


def swap(value):
    return pltpu.roll(value, N, 1)


def low_lanes(rows):
    return lax.broadcasted_iota(jnp.int32, (rows, LANES), 1) < N


def pick(first, second):
    return jnp.where(lax.axis_index("pool") == 0, first, second)


def places(unit, half):
    first, second = MEETINGS[unit]
    if second is None:
        second = OPPOSITE if half else SQUARES
    return pick(first[0], second[0]), pick(first[1], second[1])


def crossed_there():
    return (lax.axis_index("pool") == 0) | (lax.axis_index("band") >= 8)


def turned(unit, half, value):
    if not half:
        return value
    if MEETINGS[unit][1] is not None:
        return swap(value)
    return jnp.where(crossed_there(), swap(value), value)


def forward_kernel(own, near, far, table_z_far, table_y_far, out, blocks, table_z, table_y, arrived):
    copies = [
        pltpu.make_async_copy(source, target, arrived.at[at])
        for at, (source, target) in enumerate(((table_z_far, table_z), (table_y_far, table_y)))
    ]
    for copy in copies:
        copy.start()
    low = low_lanes(HALF)
    for place, (source, base) in enumerate(((own, 0), (near, 0), (near, 256), (far, 0), (far, 256))):
        for plane in range(4):
            first = source[pl.ds(base + plane, HALF, stride=4), :]
            second = source[pl.ds(base + 128 + plane, HALF, stride=4), :]
            blocks[4 * place + plane, :HALF] = jnp.where(low, first, swap(second))
            blocks[4 * place + plane, HALF:] = jnp.where(low, swap(first), second)

    def density(unit, half, plane):
        left, right = places(unit, half)
        return blocks[4 * left + plane] * turned(unit, half, blocks[4 * right + plane])

    def last_density(half, plane_low):
        if half:
            return jnp.zeros((N, LANES), jnp.float32)
        at, behind = blocks[plane_low], blocks[2 + plane_low]
        return 0.5 * jnp.where(low_lanes(N), at * swap(at), behind * swap(behind))

    def spectrum(halves_of):
        rows = jnp.concatenate(
            [jnp.concatenate([halves_of(0, at), halves_of(1, at)], axis=1) for at in range(2)], axis=0
        )
        rows = times_table(rows, table_z)
        rows = jnp.concatenate(
            [
                rows[at * N : at * N + N, part * LANES : part * LANES + LANES]
                for at in range(2)
                for part in range(2)
            ],
            axis=0,
        )
        return table_times(table_y, rows).reshape(PEERS, 16, LANES)

    for copy in copies:
        copy.wait()
    for u in range(UNITS):
        for high in range(2):
            rows = spectrum(lambda half, at: density(u, half, 2 * high + at))
            at = 32 * u + 8 * high
            out[:, at : at + 8, :] = rows[:, :8]
            out[:, at + 16 : at + 24, :] = rows[:, 8:]
    out[:, 32 * UNITS :, :] = spectrum(last_density)


def middle_kernel(spectra, kernel, table_x, table_x_back, out):
    low = low_lanes(N)
    first, second = (kernel[:, at : at + LANES] * (-1.0 / CELLS) for at in (0, LANES))

    def twice(value):
        other = swap(value)
        return jnp.where(low, value, other), jnp.where(low, other, value)

    def rows_of(pair):
        return jnp.concatenate([*pair, *pair], axis=0)

    def apply(rows, coulomb):
        rows = table_times(table_x, rows.reshape(256, LANES)) * coulomb
        return table_times(table_x_back, rows).reshape(PEERS, 16, LANES)

    coulombs = rows_of(twice(first)), rows_of(twice(second))
    for u in range(UNITS):
        for high in range(2):
            at = 32 * u + 16 * high
            out[:, at : at + 16, :] = apply(spectra[:, at : at + 16, :], coulombs[high])

    def exchanged(one, two):
        wide = lax.broadcasted_iota(jnp.int32, one.shape, 2) < N
        one_other, two_other = pltpu.roll(one, N, 2), pltpu.roll(two, N, 2)
        return jnp.where(wide, one, two_other), jnp.where(wide, one_other, two)

    at = 32 * UNITS
    rows = jnp.concatenate(
        exchanged(spectra[:, at : at + 8, :], spectra[:, at + 8 : at + 16, :]), axis=1
    )
    rows = apply(
        rows, rows_of((jnp.where(low, first, swap(second)), jnp.where(low, swap(first), second)))
    )
    one, two = exchanged(rows[:, :8], rows[:, 8:])
    out[:, at : at + 8, :] = one
    out[:, at + 8 : at + 16, :] = two


def backward_kernel(
    returned, blocks, table_y_back, table_z_back, own_field, near_fields, far_fields, fields
):
    fields[...] = jnp.zeros_like(fields)

    def collect(unit, half, plane, potential):
        left, right = places(unit, half)
        partner = turned(unit, half, blocks[4 * right + plane])
        fields[4 * left + plane] += potential * partner
        given = turned(unit, half, potential * blocks[4 * left + plane])
        if unit == UNITS - 1 and not half:
            given = given * pick(1.0, 0.0)
        fields[4 * right + plane] += given

    def potentials(rows):
        rows = table_times(table_y_back, rows.reshape(256, LANES))
        rows = jnp.concatenate(
            [
                jnp.concatenate(
                    [rows[at * LANES + part * N : at * LANES + part * N + N] for part in range(2)],
                    axis=1,
                )
                for at in range(2)
            ],
            axis=0,
        )
        return times_table(rows, table_z_back)

    for u in range(UNITS):
        for high in range(2):
            at = 32 * u + 8 * high
            rows = potentials(
                jnp.concatenate([returned[:, at : at + 8, :], returned[:, at + 16 : at + 24, :]], axis=1)
            )
            for at in range(2):
                for half in range(2):
                    collect(
                        u,
                        half,
                        2 * high + at,
                        rows[at * N : at * N + N, half * LANES : half * LANES + LANES],
                    )
    rows = potentials(returned[:, 32 * UNITS :, :])
    low = low_lanes(N)
    for at in range(2):
        potential = rows[at * N : at * N + N, :LANES]
        other = swap(potential)
        fields[at] += jnp.where(low, potential, other) * swap(blocks[at])
        fields[2 + at] += jnp.where(low, other, potential) * swap(blocks[2 + at])
    own_field[...] = fields[0:4]
    near_fields[...] = fields[4:12]
    far_fields[...] = fields[12:20]


def final_kernel(both, out):
    low = low_lanes(HALF)
    for plane in range(4):
        even, odd = (
            both[plane, at : at + HALF] + both[4 + plane, at : at + HALF] for at in (0, HALF)
        )
        out[pl.ds(plane, HALF, stride=4), :] = jnp.where(low, even, swap(odd))
        out[pl.ds(128 + plane, HALF, stride=4), :] = jnp.where(low, swap(even), odd)


VMEM = pl.BlockSpec(memory_space=pltpu.VMEM)
ANY = pl.BlockSpec(memory_space=pl.ANY)
PARAMS = pltpu.CompilerParams(vmem_limit_bytes=32 * 1024 * 1024)
CHUNKS = jax.ShapeDtypeStruct((PEERS, ROWS, LANES), jnp.float32)
TABLE = pltpu.VMEM((2, 256, 256), jnp.bfloat16)


def planes(count):
    return jax.ShapeDtypeStruct((count, N, LANES), jnp.float32)


def forward(own, near, far, table_z, table_y):
    return pl.pallas_call(
        forward_kernel,
        out_shape=[CHUNKS, planes(20)],
        in_specs=[VMEM] * 3 + [ANY] * 2,
        out_specs=[VMEM] * 2,
        scratch_shapes=[TABLE, TABLE, pltpu.SemaphoreType.DMA((2,))],
        compiler_params=PARAMS,
    )(own, near, far, table_z, table_y)


def middle(spectra, kernel, table_x, table_x_back):
    return pl.pallas_call(
        middle_kernel,
        out_shape=CHUNKS,
        in_specs=[VMEM] * 4,
        out_specs=VMEM,
        compiler_params=PARAMS,
    )(spectra, kernel, table_x, table_x_back)


def backward(returned, blocks, table_y_back, table_z_back):
    return pl.pallas_call(
        backward_kernel,
        out_shape=[planes(4), planes(8), planes(8)],
        in_specs=[VMEM] * 4,
        out_specs=[VMEM] * 3,
        scratch_shapes=[pltpu.VMEM((20, N, LANES), jnp.float32)],
        compiler_params=PARAMS,
    )(returned, blocks, table_y_back, table_z_back)


def final(both):
    return pl.pallas_call(
        final_kernel,
        out_shape=jax.ShapeDtypeStruct((256, LANES), jnp.float32),
        in_specs=[VMEM],
        out_specs=VMEM,
        compiler_params=PARAMS,
    )(both)


def along_band(value, steps):
    count = lax.axis_size("band")
    pairs = [
        (2 * source + core, 2 * ((source + steps[core]) % count) + core)
        for source in range(count)
        for core in range(2)
    ]
    return lax.ppermute(value, ("band", "pool"), pairs)


def both_cores(value):
    return lax.all_gather(value, "pool", tiled=True)


def exchange(value):
    return lax.all_to_all(value, "fft", split_axis=0, concat_axis=0, tiled=True)


def send_home(fields, steps, pool_at):
    shares = both_cores(fields).reshape(2, 2, 4, N, LANES)
    mine = lax.dynamic_index_in_dim(shares, pool_at, 1, keepdims=False)
    return along_band(mine[0] + mine[1], steps)


def local(orbitals, kernel):
    pool_at = lax.axis_index("pool")
    table_z, table_y, table_x, table_x_back, table_y_back, table_z_back = [
        jnp.asarray(t) for t in tables()
    ]
    own = orbitals.reshape(2, 4, HALF, LANES).transpose(0, 2, 1, 3).reshape(256, LANES)
    near = both_cores(along_band(own, [-s for s in NEAR]))
    far = both_cores(along_band(own, [-s for s in FAR]))
    spectra, blocks = forward(own, near, far, table_z, table_y)
    returned = exchange(middle(exchange(spectra), kernel, table_x, table_x_back))
    own_field, near_fields, far_fields = backward(returned, blocks, table_y_back, table_z_back)
    arrived = send_home(near_fields, NEAR, pool_at) + send_home(far_fields, FAR, pool_at)
    field = final(both_cores(arrived + own_field))
    return field.reshape(2, HALF, 4, LANES).transpose(0, 2, 1, 3).reshape(2, 4, N * N)


def solution(mesh):
    return jax.shard_map(
        local,
        mesh=mesh,
        in_specs=(P("band", "fft", None), P(None, "fft")),
        out_specs=P("band", "fft", None),
        check_vma=False,
    )
```

```python
import jax
import jax.numpy as jnp
import ml_dtypes
import numpy as np
from jax import lax
from jax.experimental import pallas as pl
from jax.experimental.pallas import tpu as pltpu
from jax.sharding import PartitionSpec as P

N = 64
HALF = N // 2
CELLS = N * N * N
LANES = 2 * N
PEERS = 16
UNITS = 4
ROWS = 32 * UNITS + 16

NEAR = (2, -3)
FAR = (4, -4)
MEETINGS = (((0, 1), (0, 2)), ((1, 4), (2, 3)), ((2, 4), (0, 4)), ((1, 2), None))
SQUARES = (0, 0)
OPPOSITE = (4, 3)


def wave_parts(rows, columns):
    angle = 2.0 * np.pi / N * ((rows * columns) % N)
    return np.cos(angle), np.sin(angle)


def split_table(table):
    high = table.astype(ml_dtypes.bfloat16)
    low = (table - high.astype(np.float64)).astype(ml_dtypes.bfloat16)
    return np.stack([high, low])


def tables():
    index = np.arange(N)
    cosine, sine = wave_parts(index[:, None], index[None, :])
    turn = np.stack([np.stack([cosine, sine]), np.stack([-sine, cosine])])
    two = np.eye(2)
    along_z = np.einsum("oikz,ab->iazobk", turn, two).reshape(256, 256)
    along_y = np.einsum("oiky,ab->kaoiby", turn, two)
    along_y = along_y.reshape(PEERS, 2, 2, 2, 2, 2, 2, HALF, 2)
    along_y = along_y.transpose(0, 1, 3, 4, 2, 6, 5, 8, 7).reshape(256, 256)
    along_x = np.einsum("oikx,ab->oakxib", turn, two).reshape(256, 256)
    return [split_table(t) for t in (along_z, along_y, along_x, along_x.T, along_y.T, along_z.T)]


def halves(value):
    high = value.astype(jnp.bfloat16)
    low = (value - high.astype(jnp.float32)).astype(jnp.bfloat16)
    return high, low


def dot(left, right):
    return jnp.dot(left, right, preferred_element_type=jnp.float32)


def times_table(value, table):
    high, low = halves(value)
    return dot(high, table[0]) + dot(low, table[0]) + dot(high, table[1])


def table_times(table, value):
    high, low = halves(value)
    return dot(table[0], high) + dot(table[0], low) + dot(table[1], high)


def swap(value):
    return pltpu.roll(value, N, 1)


def low_lanes(rows):
    return lax.broadcasted_iota(jnp.int32, (rows, LANES), 1) < N


def pick(first, second):
    return jnp.where(lax.axis_index("pool") == 0, first, second)


def places(unit, half):
    first, second = MEETINGS[unit]
    if second is None:
        second = OPPOSITE if half else SQUARES
    return pick(first[0], second[0]), pick(first[1], second[1])


def crossed_there():
    return (lax.axis_index("pool") == 0) | (lax.axis_index("band") >= 8)


def turned(unit, half, value):
    if not half:
        return value
    if MEETINGS[unit][1] is not None:
        return swap(value)
    return jnp.where(crossed_there(), swap(value), value)


def unfold(source, base, blocks, place):
    low = low_lanes(HALF)
    for plane in range(4):
        first = source[pl.ds(base + plane, HALF, stride=4), :]
        second = source[pl.ds(base + 128 + plane, HALF, stride=4), :]
        blocks[4 * place + plane, :HALF] = jnp.where(low, first, swap(second))
        blocks[4 * place + plane, HALF:] = jnp.where(low, swap(first), second)


def spectrum(halves_of, table_z, table_y):
    rows = jnp.concatenate(
        [jnp.concatenate([halves_of(0, at), halves_of(1, at)], axis=1) for at in range(2)], axis=0
    )
    rows = times_table(rows, table_z)
    rows = jnp.concatenate(
        [
            rows[at * N : at * N + N, part * LANES : part * LANES + LANES]
            for at in range(2)
            for part in range(2)
        ],
        axis=0,
    )
    return table_times(table_y, rows).reshape(PEERS, 16, LANES)


def first_kernel(own, table_z, table_y, blocks, last):
    unfold(own, 0, blocks, 0)

    def density(half, plane_low):
        if half:
            return jnp.zeros((N, LANES), jnp.float32)
        at, behind = blocks[plane_low], blocks[2 + plane_low]
        return 0.5 * jnp.where(low_lanes(N), at * swap(at), behind * swap(behind))

    last[...] = spectrum(density, table_z, table_y)


def forward_kernel(own_blocks, last, near, far, table_z, table_y, out, blocks):
    blocks[:4] = own_blocks[...]
    unfold(near, 0, blocks, 1)
    unfold(near, 256, blocks, 2)
    unfold(far, 0, blocks, 3)
    unfold(far, 256, blocks, 4)
    out[:, 32 * UNITS :, :] = last[...]

    def density(unit, half, plane):
        left, right = places(unit, half)
        return blocks[4 * left + plane] * turned(unit, half, blocks[4 * right + plane])

    for u in range(UNITS):
        for high in range(2):
            rows = spectrum(lambda half, at: density(u, half, 2 * high + at), table_z, table_y)
            at = 32 * u + 8 * high
            out[:, at : at + 8, :] = rows[:, :8]
            out[:, at + 16 : at + 24, :] = rows[:, 8:]


def middle_kernel(spectra, kernel, table_x, table_x_back, out):
    low = low_lanes(N)
    first, second = (kernel[:, at : at + LANES] * (-1.0 / CELLS) for at in (0, LANES))

    def twice(value):
        other = swap(value)
        return jnp.where(low, value, other), jnp.where(low, other, value)

    def rows_of(pair):
        return jnp.concatenate([*pair, *pair], axis=0)

    def apply(rows, coulomb):
        rows = table_times(table_x, rows.reshape(256, LANES)) * coulomb
        return table_times(table_x_back, rows).reshape(PEERS, 16, LANES)

    coulombs = rows_of(twice(first)), rows_of(twice(second))
    for u in range(UNITS):
        for high in range(2):
            at = 32 * u + 16 * high
            out[:, at : at + 16, :] = apply(spectra[:, at : at + 16, :], coulombs[high])

    def exchanged(one, two):
        wide = lax.broadcasted_iota(jnp.int32, one.shape, 2) < N
        one_other, two_other = pltpu.roll(one, N, 2), pltpu.roll(two, N, 2)
        return jnp.where(wide, one, two_other), jnp.where(wide, one_other, two)

    at = 32 * UNITS
    rows = jnp.concatenate(
        exchanged(spectra[:, at : at + 8, :], spectra[:, at + 8 : at + 16, :]), axis=1
    )
    rows = apply(
        rows, rows_of((jnp.where(low, first, swap(second)), jnp.where(low, swap(first), second)))
    )
    one, two = exchanged(rows[:, :8], rows[:, 8:])
    out[:, at : at + 8, :] = one
    out[:, at + 8 : at + 16, :] = two


def backward_kernel(
    returned, blocks, table_y_back, table_z_back, own_field, near_fields, far_fields, fields
):
    fields[...] = jnp.zeros_like(fields)

    def collect(unit, half, plane, potential):
        left, right = places(unit, half)
        partner = turned(unit, half, blocks[4 * right + plane])
        fields[4 * left + plane] += potential * partner
        given = turned(unit, half, potential * blocks[4 * left + plane])
        if unit == UNITS - 1 and not half:
            given = given * pick(1.0, 0.0)
        fields[4 * right + plane] += given

    def potentials(rows):
        rows = table_times(table_y_back, rows.reshape(256, LANES))
        rows = jnp.concatenate(
            [
                jnp.concatenate(
                    [rows[at * LANES + part * N : at * LANES + part * N + N] for part in range(2)],
                    axis=1,
                )
                for at in range(2)
            ],
            axis=0,
        )
        return times_table(rows, table_z_back)

    for u in range(UNITS):
        for high in range(2):
            at = 32 * u + 8 * high
            rows = potentials(
                jnp.concatenate([returned[:, at : at + 8, :], returned[:, at + 16 : at + 24, :]], axis=1)
            )
            for at in range(2):
                for half in range(2):
                    collect(
                        u,
                        half,
                        2 * high + at,
                        rows[at * N : at * N + N, half * LANES : half * LANES + LANES],
                    )
    rows = potentials(returned[:, 32 * UNITS :, :])
    low = low_lanes(N)
    for at in range(2):
        potential = rows[at * N : at * N + N, :LANES]
        other = swap(potential)
        fields[at] += jnp.where(low, potential, other) * swap(blocks[at])
        fields[2 + at] += jnp.where(low, other, potential) * swap(blocks[2 + at])
    own_field[...] = fields[0:4]
    near_fields[...] = fields[4:12]
    far_fields[...] = fields[12:20]


def share_kernel(shares, field):
    at = 4 * lax.axis_index("pool")
    for plane in range(4):
        field[plane] = shares[at + plane] + shares[8 + at + plane]


def final_kernel(both, out):
    low = low_lanes(HALF)
    for plane in range(4):
        even, odd = (
            both[plane, at : at + HALF] + both[4 + plane, at : at + HALF] for at in (0, HALF)
        )
        out[pl.ds(plane, HALF, stride=4), :] = jnp.where(low, even, swap(odd))
        out[pl.ds(128 + plane, HALF, stride=4), :] = jnp.where(low, swap(even), odd)


VMEM = pl.BlockSpec(memory_space=pltpu.VMEM)
PARAMS = pltpu.CompilerParams(vmem_limit_bytes=32 * 1024 * 1024)
CHUNKS = jax.ShapeDtypeStruct((PEERS, ROWS, LANES), jnp.float32)
LAST = jax.ShapeDtypeStruct((PEERS, 16, LANES), jnp.float32)


def planes(count):
    return jax.ShapeDtypeStruct((count, N, LANES), jnp.float32)


def first(own, table_z, table_y):
    return pl.pallas_call(
        first_kernel,
        out_shape=[planes(4), LAST],
        in_specs=[VMEM] * 3,
        out_specs=[VMEM] * 2,
        compiler_params=PARAMS,
        cost_estimate=pl.CostEstimate(flops=10**8, bytes_accessed=10**6, transcendentals=0),
    )(own, table_z, table_y)


def forward(own_blocks, last, near, far, table_z, table_y):
    return pl.pallas_call(
        forward_kernel,
        out_shape=[CHUNKS, planes(20)],
        in_specs=[VMEM] * 6,
        out_specs=[VMEM] * 2,
        compiler_params=PARAMS,
    )(own_blocks, last, near, far, table_z, table_y)


def middle(spectra, kernel, table_x, table_x_back):
    return pl.pallas_call(
        middle_kernel,
        out_shape=CHUNKS,
        in_specs=[VMEM] * 4,
        out_specs=VMEM,
        compiler_params=PARAMS,
    )(spectra, kernel, table_x, table_x_back)


def backward(returned, blocks, table_y_back, table_z_back):
    return pl.pallas_call(
        backward_kernel,
        out_shape=[planes(4), planes(8), planes(8)],
        in_specs=[VMEM] * 4,
        out_specs=[VMEM] * 3,
        scratch_shapes=[pltpu.VMEM((20, N, LANES), jnp.float32)],
        compiler_params=PARAMS,
    )(returned, blocks, table_y_back, table_z_back)


def share(fields):
    return pl.pallas_call(
        share_kernel,
        out_shape=planes(4),
        in_specs=[VMEM],
        out_specs=VMEM,
        compiler_params=PARAMS,
    )(both_cores(fields))


def final(both):
    return pl.pallas_call(
        final_kernel,
        out_shape=jax.ShapeDtypeStruct((256, LANES), jnp.float32),
        in_specs=[VMEM],
        out_specs=VMEM,
        compiler_params=PARAMS,
    )(both)


def along_band(value, steps):
    count = lax.axis_size("band")
    pairs = [
        (2 * source + core, 2 * ((source + steps[core]) % count) + core)
        for source in range(count)
        for core in range(2)
    ]
    return lax.ppermute(value, ("band", "pool"), pairs)


def both_cores(value):
    return lax.all_gather(value, "pool", tiled=True)


def exchange(value):
    return lax.all_to_all(value, "fft", split_axis=0, concat_axis=0, tiled=True)


def local(orbitals, kernel):
    table_z, table_y, table_x, table_x_back, table_y_back, table_z_back = [
        jnp.asarray(t) for t in tables()
    ]
    own = orbitals.reshape(2, 4, HALF, LANES).transpose(0, 2, 1, 3).reshape(256, LANES)
    far = both_cores(along_band(own, [-s for s in FAR]))
    near = both_cores(along_band(own, [-s for s in NEAR]))
    own_blocks, last = first(own, table_z, table_y)
    spectra, blocks = forward(own_blocks, last, near, far, table_z, table_y)
    returned = exchange(middle(exchange(spectra), kernel, table_x, table_x_back))
    own_field, near_fields, far_fields = backward(returned, blocks, table_y_back, table_z_back)
    far_field = along_band(share(far_fields), FAR)
    near_field = along_band(share(near_fields), NEAR)
    field = final(both_cores(far_field + near_field + own_field))
    return field.reshape(2, HALF, 4, LANES).transpose(0, 2, 1, 3).reshape(2, 4, N * N)


def solution(mesh):
    return jax.shard_map(
        local,
        mesh=mesh,
        in_specs=(P("band", "fft", None), P(None, "fft")),
        out_specs=P("band", "fft", None),
        check_vma=False,
    )
```

```python
import jax
import jax.numpy as jnp
import ml_dtypes
import numpy as np
from jax import lax
from jax.experimental import pallas as pl
from jax.experimental.pallas import tpu as pltpu
from jax.sharding import PartitionSpec as P

N = 64
HALF = N // 2
CELLS = N * N * N
LANES = 2 * N
PEERS = 16
UNITS = 4
ROWS = 32 * UNITS + 16

FAR = (-5, 4)
NEAR = (3, -2)
MEETINGS = (((0, 1), (0, 1)), ((0, 2), (0, 2)), ((1, 2), (1, 2)), ((2, 3), (1, 3)))
EIGHT = 2


def wave_parts(rows, columns):
    angle = 2.0 * np.pi / N * ((rows * columns) % N)
    return np.cos(angle), np.sin(angle)


def split_table(table):
    high = table.astype(ml_dtypes.bfloat16)
    low = (table - high.astype(np.float64)).astype(ml_dtypes.bfloat16)
    return np.stack([high, low])


def tables():
    index = np.arange(N)
    cosine, sine = wave_parts(index[:, None], index[None, :])
    turn = np.stack([np.stack([cosine, sine]), np.stack([-sine, cosine])])
    two = np.eye(2)
    along_z = np.einsum("oikz,ab->iazobk", turn, two).reshape(256, 256)
    along_y = np.einsum("oiky,ab->kaoiby", turn, two)
    along_y = along_y.reshape(PEERS, 2, 2, 2, 2, 2, 2, HALF, 2)
    along_y = along_y.transpose(0, 1, 3, 4, 2, 6, 5, 8, 7).reshape(256, 256)
    along_x = np.einsum("oikx,ab->oakxib", turn, two).reshape(256, 256)
    return [split_table(t) for t in (along_z, along_y, along_x, along_x.T, along_y.T, along_z.T)]


def halves(value):
    high = value.astype(jnp.bfloat16)
    low = (value - high.astype(jnp.float32)).astype(jnp.bfloat16)
    return high, low


def dot(left, right):
    return jnp.dot(left, right, preferred_element_type=jnp.float32)


def times_table(value, table):
    high, low = halves(value)
    return dot(high, table[0]) + dot(low, table[0]) + dot(high, table[1])


def table_times(table, value):
    high, low = halves(value)
    return dot(table[0], high) + dot(table[0], low) + dot(table[1], high)


def swap(value):
    return pltpu.roll(value, N, 1)


def low_lanes(rows):
    return lax.broadcasted_iota(jnp.int32, (rows, LANES), 1) < N


def on_first():
    return lax.axis_index("pool") == 0


def pick(first, second):
    return first if first is second else jnp.where(on_first(), first, second)


def places(unit, half):
    first, second = MEETINGS[unit]
    if unit == EIGHT and half:
        first = (0, 0)
    return pick(first[0], second[0]), pick(first[1], second[1])


def turned(unit, half, value):
    if unit == EIGHT:
        late = lax.axis_index("band") >= 8
        crossed = jnp.logical_not(on_first()) if half else on_first() & late
        return jnp.where(crossed, swap(value), value)
    return swap(value) if half else value


def reader(own_blocks, blocks):
    def read(place, plane):
        if isinstance(place, int):
            return blocks[4 * place - 4 + plane] if place else own_blocks[plane]
        return blocks[4 * place - 4 + plane]

    return read


def unfold(source, base, blocks, place):
    low = low_lanes(HALF)
    for plane in range(4):
        first = source[pl.ds(base + plane, HALF, stride=4), :]
        second = source[pl.ds(base + 128 + plane, HALF, stride=4), :]
        blocks[4 * place + plane, :HALF] = jnp.where(low, first, swap(second))
        blocks[4 * place + plane, HALF:] = jnp.where(low, swap(first), second)


def first_kernel(own, blocks):
    unfold(own, 0, blocks, 0)


def spectrum(density, table_z, table_y):
    rows = times_table(jnp.concatenate(density, axis=0), table_z)
    pairs = [
        jnp.concatenate(
            [
                rows[base + at * N : base + at * N + N, part * LANES : part * LANES + LANES]
                for at in range(2)
                for part in range(2)
            ],
            axis=0,
        )
        for base in range(0, rows.shape[0], LANES)
    ]
    rows = jnp.concatenate(pairs, axis=1)
    return table_times(table_y, rows).reshape(PEERS, 16, rows.shape[1])


def forward_kernel(own_blocks, far, near, table_z, table_y, out, blocks):
    core = lax.axis_index("pool")
    unfold(far, 256 * core, blocks, 0)
    unfold(near, 0, blocks, 1)
    unfold(far, 256 * (1 - core), blocks, 2)
    read = reader(own_blocks, blocks)

    def density(unit, half, plane):
        left, right = places(unit, half)
        if unit == EIGHT and half:
            left = jnp.where(on_first(), read(0, plane), read(1, plane))
            right = jnp.where(on_first(), read(0, plane), swap(read(2, plane)))
            return left * right
        return read(left, plane) * turned(unit, half, read(right, plane))

    for u in range(UNITS):
        rows = spectrum(
            [
                jnp.concatenate([density(u, 0, plane), density(u, 1, plane)], axis=1)
                for plane in range(4)
            ],
            table_z,
            table_y,
        )
        for ky_high in range(2):
            for high in range(2):
                at = 32 * u + 16 * ky_high + 8 * high
                out[:, at : at + 8, :] = rows[
                    :, 8 * ky_high : 8 * ky_high + 8, LANES * high : LANES * high + LANES
                ]

    last = []
    for at, behind in ((own_blocks[0], own_blocks[2]), (own_blocks[1], own_blocks[3])):
        pairs = 0.5 * jnp.where(low_lanes(N), at * swap(at), behind * swap(behind))
        last.append(jnp.concatenate([pairs, jnp.zeros((N, LANES), jnp.float32)], axis=1))
    out[:, 32 * UNITS :, :] = spectrum(last, table_z, table_y)


def middle_kernel(spectra, kernel, table_x, table_x_back, out):
    low = low_lanes(N)
    first, second = (kernel[:, at : at + LANES] * (-1.0 / CELLS) for at in (0, LANES))

    def twice(value):
        other = swap(value)
        return jnp.where(low, value, other), jnp.where(low, other, value)

    def rows_of(pair):
        return jnp.concatenate([*pair, *pair], axis=0)

    def apply(rows, coulomb):
        return table_times(table_x_back, table_times(table_x, rows) * coulomb)

    coulombs = jnp.concatenate([rows_of(twice(first)), rows_of(twice(second))], axis=1)
    for u in range(UNITS):
        starts = 32 * u, 32 * u + 16
        rows = jnp.concatenate(
            [spectra[:, at : at + 16, :].reshape(256, LANES) for at in starts], axis=1
        )
        rows = apply(rows, coulombs)
        for part, at in enumerate(starts):
            out[:, at : at + 16, :] = rows[:, part * LANES : part * LANES + LANES].reshape(
                PEERS, 16, LANES
            )

    def exchanged(one, two):
        wide = lax.broadcasted_iota(jnp.int32, one.shape, 2) < N
        one_other, two_other = pltpu.roll(one, N, 2), pltpu.roll(two, N, 2)
        return jnp.where(wide, one, two_other), jnp.where(wide, one_other, two)

    at = 32 * UNITS
    rows = jnp.concatenate(
        exchanged(spectra[:, at : at + 8, :], spectra[:, at + 8 : at + 16, :]), axis=1
    )
    rows = apply(
        rows.reshape(256, LANES),
        rows_of((jnp.where(low, first, swap(second)), jnp.where(low, swap(first), second))),
    ).reshape(PEERS, 16, LANES)
    one, two = exchanged(rows[:, :8], rows[:, 8:])
    out[:, at : at + 8, :] = one
    out[:, at + 8 : at + 16, :] = two


def backward_kernel(
    returned,
    own_blocks,
    blocks,
    table_y_back,
    table_z_back,
    own_field,
    far_field,
    near_field,
    other_field,
    fields,
):
    fields[...] = jnp.zeros_like(fields)
    read = reader(own_blocks, blocks)

    def collect(unit, half, plane, potential):
        if unit == EIGHT and half:
            first = on_first()
            partner = jnp.where(first, read(0, plane), swap(read(2, plane)))
            mine = potential * partner
            fields[plane] += jnp.where(first, mine, 0.0)
            fields[4 + plane] += jnp.where(first, 0.0, mine)
            given = swap(potential * read(1, plane))
            fields[8 + plane] += jnp.where(first, 0.0, given)
            return
        left, right = places(unit, half)
        fields[4 * left + plane] += potential * turned(unit, half, read(right, plane))
        fields[4 * right + plane] += turned(unit, half, potential * read(left, plane))

    def potentials(pairs):
        rows = table_times(table_y_back, jnp.concatenate(pairs, axis=1))
        planes_of = [
            jnp.concatenate(
                [
                    rows[
                        at * LANES + part * N : at * LANES + part * N + N,
                        high * LANES : high * LANES + LANES,
                    ]
                    for part in range(2)
                ],
                axis=1,
            )
            for high in range(len(pairs))
            for at in range(2)
        ]
        return times_table(jnp.concatenate(planes_of, axis=0), table_z_back)

    for u in range(UNITS):
        pairs = []
        for high in range(2):
            at = 32 * u + 8 * high
            both = [returned[:, at : at + 8, :], returned[:, at + 16 : at + 24, :]]
            pairs.append(jnp.concatenate(both, axis=1).reshape(256, LANES))
        rows = potentials(pairs)
        for plane in range(4):
            for half in range(2):
                collect(
                    u,
                    half,
                    plane,
                    rows[plane * N : plane * N + N, half * LANES : half * LANES + LANES],
                )
    rows = potentials([returned[:, 32 * UNITS :, :].reshape(256, LANES)])
    low = low_lanes(N)
    for at in range(2):
        potential = rows[at * N : at * N + N, :LANES]
        other = swap(potential)
        fields[at] += jnp.where(low, potential, other) * swap(own_blocks[at])
        fields[2 + at] += jnp.where(low, other, potential) * swap(own_blocks[2 + at])
    for place, field in enumerate((own_field, far_field, near_field, other_field)):
        field[...] = fields[4 * place : 4 * place + 4]


def share_kernel(mine, others, field):
    at = 4 * (1 - lax.axis_index("pool"))
    for plane in range(4):
        field[plane] = mine[plane] + others[at + plane]


def final_kernel(both, out):
    low = low_lanes(HALF)
    for plane in range(4):
        even, odd = (
            both[plane, at : at + HALF] + both[4 + plane, at : at + HALF] for at in (0, HALF)
        )
        out[pl.ds(plane, HALF, stride=4), :] = jnp.where(low, even, swap(odd))
        out[pl.ds(128 + plane, HALF, stride=4), :] = jnp.where(low, swap(even), odd)


VMEM = pl.BlockSpec(memory_space=pltpu.VMEM)
PARAMS = pltpu.CompilerParams(vmem_limit_bytes=32 * 1024 * 1024)
CHUNKS = jax.ShapeDtypeStruct((PEERS, ROWS, LANES), jnp.float32)


def planes(count):
    return jax.ShapeDtypeStruct((count, N, LANES), jnp.float32)


def first(own):
    return pl.pallas_call(
        first_kernel,
        out_shape=planes(4),
        in_specs=[VMEM],
        out_specs=VMEM,
        compiler_params=PARAMS,
        cost_estimate=pl.CostEstimate(flops=10**10, bytes_accessed=10**6, transcendentals=0),
    )(own)


def forward(own_blocks, far, near, table_z, table_y):
    return pl.pallas_call(
        forward_kernel,
        out_shape=[CHUNKS, planes(12)],
        in_specs=[VMEM] * 5,
        out_specs=[VMEM] * 2,
        compiler_params=PARAMS,
    )(own_blocks, far, near, table_z, table_y)


def middle(spectra, kernel, table_x, table_x_back):
    return pl.pallas_call(
        middle_kernel,
        out_shape=CHUNKS,
        in_specs=[VMEM] * 4,
        out_specs=VMEM,
        compiler_params=PARAMS,
    )(spectra, kernel, table_x, table_x_back)


def backward(returned, own_blocks, blocks, table_y_back, table_z_back):
    return pl.pallas_call(
        backward_kernel,
        out_shape=[planes(4)] * 4,
        in_specs=[VMEM] * 5,
        out_specs=[VMEM] * 4,
        scratch_shapes=[pltpu.VMEM((16, N, LANES), jnp.float32)],
        compiler_params=PARAMS,
    )(returned, own_blocks, blocks, table_y_back, table_z_back)


def share(mine, others):
    return pl.pallas_call(
        share_kernel,
        out_shape=planes(4),
        in_specs=[VMEM] * 2,
        out_specs=VMEM,
        compiler_params=PARAMS,
    )(mine, others)


def final(both):
    return pl.pallas_call(
        final_kernel,
        out_shape=jax.ShapeDtypeStruct((256, LANES), jnp.float32),
        in_specs=[VMEM],
        out_specs=VMEM,
        compiler_params=PARAMS,
    )(both)


def along_band(value, steps):
    count = lax.axis_size("band")
    pairs = [
        (2 * source + core, 2 * ((source + steps[core]) % count) + core)
        for source in range(count)
        for core in range(2)
    ]
    return lax.ppermute(value, ("band", "pool"), pairs)


def both_cores(value):
    return lax.all_gather(value, "pool", tiled=True)


def exchange(value):
    return lax.all_to_all(value, "fft", split_axis=0, concat_axis=0, tiled=True)


def local(orbitals, kernel):
    table_z, table_y, table_x, table_x_back, table_y_back, table_z_back = [
        jnp.asarray(t) for t in tables()
    ]
    own = orbitals.reshape(2, 4, HALF, LANES).transpose(0, 2, 1, 3).reshape(256, LANES)
    far = both_cores(along_band(own, [-s for s in FAR]))
    near = along_band(own, [-s for s in NEAR])
    own_blocks = first(own)
    spectra, blocks = forward(own_blocks, far, near, table_z, table_y)
    returned = exchange(middle(exchange(spectra), kernel, table_x, table_x_back))
    own_field, far_field, near_field, other_field = backward(
        returned, own_blocks, blocks, table_y_back, table_z_back
    )
    near_field = along_band(near_field, NEAR)
    far_field = along_band(share(far_field, both_cores(other_field)), FAR)
    field = final(both_cores(far_field + near_field + own_field))
    return field.reshape(2, HALF, 4, LANES).transpose(0, 2, 1, 3).reshape(2, 4, N * N)


def solution(mesh):
    return jax.shard_map(
        local,
        mesh=mesh,
        in_specs=(P("band", "fft", None), P(None, "fft")),
        out_specs=P("band", "fft", None),
        check_vma=False,
    )
```

```python
import jax
import jax.numpy as jnp
import ml_dtypes
import numpy as np
from jax import lax
from jax.experimental import pallas as pl
from jax.experimental.pallas import tpu as pltpu
from jax.sharding import PartitionSpec as P

N = 64
HALF = N // 2
CELLS = N * N * N
LANES = 2 * N
PEERS = 16
UNITS = 4
ROWS = 32 * UNITS + 16

FAR = (-5, 4)
NEAR = (3, -2)
MEETINGS = (((0, 1), (0, 1)), ((0, 2), (0, 2)), ((1, 2), (1, 2)), ((2, 3), (1, 3)))
EIGHT = 2


def wave_parts(rows, columns):
    angle = 2.0 * np.pi / N * ((rows * columns) % N)
    return np.cos(angle), np.sin(angle)


def split_table(table):
    high = table.astype(ml_dtypes.bfloat16)
    low = (table - high.astype(np.float64)).astype(ml_dtypes.bfloat16)
    return np.stack([high, low])


def tables():
    index = np.arange(N)
    cosine, sine = wave_parts(index[:, None], index[None, :])
    turn = np.stack([np.stack([cosine, sine]), np.stack([-sine, cosine])])
    two = np.eye(2)
    along_z = np.einsum("oikz,ab->iazobk", turn, two).reshape(256, 256)
    along_y = np.einsum("oiky,ab->kaoiby", turn, two)
    along_y = along_y.reshape(PEERS, 2, 2, 2, 2, 2, 2, HALF, 2)
    along_y = along_y.transpose(0, 1, 3, 4, 2, 6, 5, 8, 7).reshape(256, 256)
    along_x = np.einsum("oikx,ab->oakxib", turn, two).reshape(256, 256)
    return [split_table(t) for t in (along_z, along_y, along_x, along_x.T, along_y.T, along_z.T)]


def halves(value):
    high = value.astype(jnp.bfloat16)
    low = (value - high.astype(jnp.float32)).astype(jnp.bfloat16)
    return high, low


def dot(left, right):
    return jnp.dot(left, right, preferred_element_type=jnp.float32)


def times_table(value, table):
    high, low = halves(value)
    return dot(high, table[0]) + dot(low, table[0]) + dot(high, table[1])


def table_times(table, value):
    high, low = halves(value)
    return dot(table[0], high) + dot(table[0], low) + dot(table[1], high)


def swap(value):
    return pltpu.roll(value, N, 1)


def low_lanes(rows):
    return lax.broadcasted_iota(jnp.int32, (rows, LANES), 1) < N


def on_first():
    return lax.axis_index("pool") == 0


def pick(first, second):
    return first if first is second else jnp.where(on_first(), first, second)


def places(unit, half):
    first, second = MEETINGS[unit]
    if unit == EIGHT and half:
        first = (0, 0)
    return pick(first[0], second[0]), pick(first[1], second[1])


def turned(unit, half, value):
    if unit == EIGHT:
        late = lax.axis_index("band") >= 8
        crossed = jnp.logical_not(on_first()) if half else on_first() & late
        return jnp.where(crossed, swap(value), value)
    return swap(value) if half else value


def reader(own_blocks, blocks):
    def read(place, plane):
        if isinstance(place, int):
            return blocks[4 * place - 4 + plane] if place else own_blocks[plane]
        return blocks[4 * place - 4 + plane]

    return read


def unfold(source, base, blocks, place):
    low = low_lanes(HALF)
    for plane in range(4):
        first = source[pl.ds(base + plane, HALF, stride=4), :]
        second = source[pl.ds(base + 128 + plane, HALF, stride=4), :]
        blocks[4 * place + plane, :HALF] = jnp.where(low, first, swap(second))
        blocks[4 * place + plane, HALF:] = jnp.where(low, swap(first), second)


def first_kernel(own, blocks, again):
    unfold(own, 0, blocks, 0)
    again[...] = own[...]


def again_kernel(value, again):
    again[...] = value[...]


def spectrum(density, table_z, table_y):
    rows = times_table(jnp.concatenate(density, axis=0), table_z)
    pairs = [
        jnp.concatenate(
            [
                rows[base + at * N : base + at * N + N, part * LANES : part * LANES + LANES]
                for at in range(2)
                for part in range(2)
            ],
            axis=0,
        )
        for base in range(0, rows.shape[0], LANES)
    ]
    rows = jnp.concatenate(pairs, axis=1)
    return table_times(table_y, rows).reshape(PEERS, 16, rows.shape[1])


def forward_kernel(own_blocks, far, near, table_z, table_y, out, blocks):
    core = lax.axis_index("pool")
    unfold(far, 256 * core, blocks, 0)
    unfold(near, 0, blocks, 1)
    unfold(far, 256 * (1 - core), blocks, 2)
    read = reader(own_blocks, blocks)

    def density(unit, half, plane):
        left, right = places(unit, half)
        if unit == EIGHT and half:
            left = jnp.where(on_first(), read(0, plane), read(1, plane))
            right = jnp.where(on_first(), read(0, plane), swap(read(2, plane)))
            return left * right
        return read(left, plane) * turned(unit, half, read(right, plane))

    for u in range(UNITS):
        rows = spectrum(
            [
                jnp.concatenate([density(u, 0, plane), density(u, 1, plane)], axis=1)
                for plane in range(4)
            ],
            table_z,
            table_y,
        )
        for ky_high in range(2):
            for high in range(2):
                at = 32 * u + 16 * ky_high + 8 * high
                out[:, at : at + 8, :] = rows[
                    :, 8 * ky_high : 8 * ky_high + 8, LANES * high : LANES * high + LANES
                ]

    last = []
    for at, behind in ((own_blocks[0], own_blocks[2]), (own_blocks[1], own_blocks[3])):
        pairs = 0.5 * jnp.where(low_lanes(N), at * swap(at), behind * swap(behind))
        last.append(jnp.concatenate([pairs, jnp.zeros((N, LANES), jnp.float32)], axis=1))
    out[:, 32 * UNITS :, :] = spectrum(last, table_z, table_y)


def middle_kernel(spectra, kernel, table_x, table_x_back, out):
    low = low_lanes(N)
    first, second = (kernel[:, at : at + LANES] * (-1.0 / CELLS) for at in (0, LANES))

    def twice(value):
        other = swap(value)
        return jnp.where(low, value, other), jnp.where(low, other, value)

    def rows_of(pair):
        return jnp.concatenate([*pair, *pair], axis=0)

    def apply(rows, coulomb):
        return table_times(table_x_back, table_times(table_x, rows) * coulomb)

    coulombs = jnp.concatenate([rows_of(twice(first)), rows_of(twice(second))], axis=1)
    for u in range(UNITS):
        starts = 32 * u, 32 * u + 16
        rows = jnp.concatenate(
            [spectra[:, at : at + 16, :].reshape(256, LANES) for at in starts], axis=1
        )
        rows = apply(rows, coulombs)
        for part, at in enumerate(starts):
            out[:, at : at + 16, :] = rows[:, part * LANES : part * LANES + LANES].reshape(
                PEERS, 16, LANES
            )

    def exchanged(one, two):
        wide = lax.broadcasted_iota(jnp.int32, one.shape, 2) < N
        one_other, two_other = pltpu.roll(one, N, 2), pltpu.roll(two, N, 2)
        return jnp.where(wide, one, two_other), jnp.where(wide, one_other, two)

    at = 32 * UNITS
    rows = jnp.concatenate(
        exchanged(spectra[:, at : at + 8, :], spectra[:, at + 8 : at + 16, :]), axis=1
    )
    rows = apply(
        rows.reshape(256, LANES),
        rows_of((jnp.where(low, first, swap(second)), jnp.where(low, swap(first), second))),
    ).reshape(PEERS, 16, LANES)
    one, two = exchanged(rows[:, :8], rows[:, 8:])
    out[:, at : at + 8, :] = one
    out[:, at + 8 : at + 16, :] = two


def backward_kernel(
    returned,
    own_blocks,
    blocks,
    table_y_back,
    table_z_back,
    own_field,
    far_field,
    near_field,
    other_field,
    fields,
):
    fields[...] = jnp.zeros_like(fields)
    read = reader(own_blocks, blocks)

    def collect(unit, half, plane, potential):
        if unit == EIGHT and half:
            first = on_first()
            partner = jnp.where(first, read(0, plane), swap(read(2, plane)))
            mine = potential * partner
            fields[plane] += jnp.where(first, mine, 0.0)
            fields[4 + plane] += jnp.where(first, 0.0, mine)
            given = swap(potential * read(1, plane))
            fields[8 + plane] += jnp.where(first, 0.0, given)
            return
        left, right = places(unit, half)
        fields[4 * left + plane] += potential * turned(unit, half, read(right, plane))
        fields[4 * right + plane] += turned(unit, half, potential * read(left, plane))

    def potentials(pairs):
        rows = table_times(table_y_back, jnp.concatenate(pairs, axis=1))
        planes_of = [
            jnp.concatenate(
                [
                    rows[
                        at * LANES + part * N : at * LANES + part * N + N,
                        high * LANES : high * LANES + LANES,
                    ]
                    for part in range(2)
                ],
                axis=1,
            )
            for high in range(len(pairs))
            for at in range(2)
        ]
        return times_table(jnp.concatenate(planes_of, axis=0), table_z_back)

    for u in range(UNITS):
        pairs = []
        for high in range(2):
            at = 32 * u + 8 * high
            both = [returned[:, at : at + 8, :], returned[:, at + 16 : at + 24, :]]
            pairs.append(jnp.concatenate(both, axis=1).reshape(256, LANES))
        rows = potentials(pairs)
        for plane in range(4):
            for half in range(2):
                collect(
                    u,
                    half,
                    plane,
                    rows[plane * N : plane * N + N, half * LANES : half * LANES + LANES],
                )
    rows = potentials([returned[:, 32 * UNITS :, :].reshape(256, LANES)])
    low = low_lanes(N)
    for at in range(2):
        potential = rows[at * N : at * N + N, :LANES]
        other = swap(potential)
        fields[at] += jnp.where(low, potential, other) * swap(own_blocks[at])
        fields[2 + at] += jnp.where(low, other, potential) * swap(own_blocks[2 + at])
    for place, field in enumerate((own_field, far_field, near_field, other_field)):
        field[...] = fields[4 * place : 4 * place + 4]


def share_kernel(mine, near, others, field, near_again):
    near_again[...] = near[...]
    at = 4 * (1 - lax.axis_index("pool"))
    for plane in range(4):
        field[plane] = mine[plane] + others[at + plane]


def final_kernel(both, out):
    low = low_lanes(HALF)
    for plane in range(4):
        even, odd = (
            both[plane, at : at + HALF] + both[4 + plane, at : at + HALF] for at in (0, HALF)
        )
        out[pl.ds(plane, HALF, stride=4), :] = jnp.where(low, even, swap(odd))
        out[pl.ds(128 + plane, HALF, stride=4), :] = jnp.where(low, swap(even), odd)


VMEM = pl.BlockSpec(memory_space=pltpu.VMEM)
PARAMS = pltpu.CompilerParams(vmem_limit_bytes=32 * 1024 * 1024)
CHUNKS = jax.ShapeDtypeStruct((PEERS, ROWS, LANES), jnp.float32)


def planes(count):
    return jax.ShapeDtypeStruct((count, N, LANES), jnp.float32)


LONG = pl.CostEstimate(flops=10**10, bytes_accessed=10**6, transcendentals=0)


def first(own):
    return pl.pallas_call(
        first_kernel,
        out_shape=[planes(4), jax.ShapeDtypeStruct((256, LANES), jnp.float32)],
        in_specs=[VMEM],
        out_specs=[VMEM] * 2,
        compiler_params=PARAMS,
        cost_estimate=LONG,
    )(own)


def again(value):
    return pl.pallas_call(
        again_kernel,
        out_shape=planes(4),
        in_specs=[VMEM],
        out_specs=VMEM,
        compiler_params=PARAMS,
        cost_estimate=LONG,
    )(value)


def forward(own_blocks, far, near, table_z, table_y):
    return pl.pallas_call(
        forward_kernel,
        out_shape=[CHUNKS, planes(12)],
        in_specs=[VMEM] * 5,
        out_specs=[VMEM] * 2,
        compiler_params=PARAMS,
    )(own_blocks, far, near, table_z, table_y)


def middle(spectra, kernel, table_x, table_x_back):
    return pl.pallas_call(
        middle_kernel,
        out_shape=CHUNKS,
        in_specs=[VMEM] * 4,
        out_specs=VMEM,
        compiler_params=PARAMS,
    )(spectra, kernel, table_x, table_x_back)


def backward(returned, own_blocks, blocks, table_y_back, table_z_back):
    return pl.pallas_call(
        backward_kernel,
        out_shape=[planes(4)] * 4,
        in_specs=[VMEM] * 5,
        out_specs=[VMEM] * 4,
        scratch_shapes=[pltpu.VMEM((16, N, LANES), jnp.float32)],
        compiler_params=PARAMS,
    )(returned, own_blocks, blocks, table_y_back, table_z_back)


def share(mine, near, others):
    return pl.pallas_call(
        share_kernel,
        out_shape=[planes(4)] * 2,
        in_specs=[VMEM] * 3,
        out_specs=[VMEM] * 2,
        compiler_params=PARAMS,
    )(mine, near, others)


def final(both):
    return pl.pallas_call(
        final_kernel,
        out_shape=jax.ShapeDtypeStruct((256, LANES), jnp.float32),
        in_specs=[VMEM],
        out_specs=VMEM,
        compiler_params=PARAMS,
    )(both)


def along_band(value, steps):
    count = lax.axis_size("band")
    pairs = [
        (2 * source + core, 2 * ((source + steps[core]) % count) + core)
        for source in range(count)
        for core in range(2)
    ]
    return lax.ppermute(value, ("band", "pool"), pairs)


def both_cores(value):
    return lax.all_gather(value, "pool", tiled=True)


def exchange(value):
    return lax.all_to_all(value, "fft", split_axis=0, concat_axis=0, tiled=True)


def local(orbitals, kernel):
    table_z, table_y, table_x, table_x_back, table_y_back, table_z_back = [
        jnp.asarray(t) for t in tables()
    ]
    own = orbitals.reshape(2, 4, HALF, LANES).transpose(0, 2, 1, 3).reshape(256, LANES)
    far = both_cores(along_band(own, [-s for s in FAR]))
    own_blocks, own_again = first(own)
    near = along_band(own_again, [-s for s in NEAR])
    spectra, blocks = forward(own_blocks, far, near, table_z, table_y)
    returned = exchange(middle(exchange(spectra), kernel, table_x, table_x_back))
    own_field, far_field, near_field, other_field = backward(
        returned, own_blocks, blocks, table_y_back, table_z_back
    )
    far_field, near_field = share(far_field, near_field, both_cores(other_field))
    far_field = along_band(again(far_field), FAR)
    near_field = along_band(near_field, NEAR)
    field = final(both_cores(near_field + far_field + own_field))
    return field.reshape(2, HALF, 4, LANES).transpose(0, 2, 1, 3).reshape(2, 4, N * N)


def solution(mesh):
    return jax.shard_map(
        local,
        mesh=mesh,
        in_specs=(P("band", "fft", None), P(None, "fft")),
        out_specs=P("band", "fft", None),
        check_vma=False,
    )
```

```python
import jax
import jax.numpy as jnp
import ml_dtypes
import numpy as np
from jax import lax
from jax.experimental import pallas as pl
from jax.experimental.pallas import tpu as pltpu
from jax.sharding import PartitionSpec as P

N = 64
HALF = N // 2
CELLS = N * N * N
LANES = 2 * N
PEERS = 16
UNITS = 4
ROWS = 32 * UNITS + 8

SHARED = (-3, 4)
ALONE = (-2, 5)
RELAY = tuple(lone - shared for lone, shared in zip(ALONE, SHARED))
MEETINGS = (((0, 2), (0, 2)), ((0, 1), (0, 1)), ((1, 2), (1, 3)), ((2, 3), (2, 3)))
EIGHT = 3
EIGHT_CORE = 1


def wave_parts(rows, columns):
    angle = 2.0 * np.pi / N * ((rows * columns) % N)
    return np.cos(angle), np.sin(angle)


def split_table(table):
    high = table.astype(ml_dtypes.bfloat16)
    low = (table - high.astype(np.float64)).astype(ml_dtypes.bfloat16)
    return np.stack([high, low])


def tables():
    index = np.arange(N)
    cosine, sine = wave_parts(index[:, None], index[None, :])
    turn = np.stack([np.stack([cosine, sine]), np.stack([-sine, cosine])])
    two = np.eye(2)
    along_z = np.einsum("oikz,ab->iazobk", turn, two).reshape(256, 256)
    along_y = np.einsum("oiky,ab->kaoiby", turn, two)
    along_y = along_y.reshape(PEERS, 2, 2, 2, 2, 2, 2, HALF, 2)
    along_y = along_y.transpose(0, 1, 4, 3, 2, 6, 5, 8, 7).reshape(256, 256)
    along_x = np.einsum("oikx,ab->oakxib", turn, two).reshape(2, 2, N, HALF, 2, 2, 2)
    along_x = along_x.transpose(0, 1, 2, 3, 5, 4, 6).reshape(256, 256)
    return [split_table(t) for t in (along_z, along_y, along_x, along_x.T, along_y.T, along_z.T)]


def halves(value):
    high = value.astype(jnp.bfloat16)
    low = (value - high.astype(jnp.float32)).astype(jnp.bfloat16)
    return high, low


def dot(left, right):
    return jnp.dot(left, right, preferred_element_type=jnp.float32)


def times_table(value, table):
    high, low = halves(value)
    return dot(high, table[0]) + dot(low, table[0]) + dot(high, table[1])


def table_times(table, value):
    high, low = halves(value)
    return dot(table[0], high) + dot(table[0], low) + dot(table[1], high)


def swap(value):
    return pltpu.roll(value, N, 1)


def low_lanes(rows):
    return lax.broadcasted_iota(jnp.int32, (rows, LANES), 1) < N


def on_first():
    return lax.axis_index("pool") == 0


def on_eight():
    return lax.axis_index("pool") == EIGHT_CORE


def pick(first, second):
    return first if first is second else jnp.where(on_first(), first, second)


def places(unit):
    first, second = MEETINGS[unit]
    return pick(first[0], second[0]), pick(first[1], second[1])


def turned(unit, half, value):
    if unit == EIGHT and not half:
        return jnp.where(on_eight() & (lax.axis_index("band") >= 8), swap(value), value)
    return swap(value) if half else value


def reader(own_blocks, blocks):
    def read(place, plane):
        if isinstance(place, int):
            return blocks[4 * place - 4 + plane] if place else own_blocks[plane]
        return blocks[4 * place - 4 + plane]

    return read


def unfold(source, base, blocks, place):
    low = low_lanes(HALF)
    for plane in range(4):
        first = source[pl.ds(base + plane, HALF, stride=4), :]
        second = source[pl.ds(base + 128 + plane, HALF, stride=4), :]
        blocks[4 * place + plane, :HALF] = jnp.where(low, first, swap(second))
        blocks[4 * place + plane, HALF:] = jnp.where(low, swap(first), second)


def first_kernel(own, blocks, again):
    unfold(own, 0, blocks, 0)
    again[...] = own[...]


def spectrum(density, table_z, table_y):
    rows = times_table(jnp.concatenate(density, axis=0), table_z)
    pairs = [
        jnp.concatenate(
            [
                rows[base + at * N : base + at * N + N, part * LANES : part * LANES + LANES]
                for at in range(2)
                for part in range(2)
            ],
            axis=0,
        )
        for base in range(0, rows.shape[0], LANES)
    ]
    rows = jnp.concatenate(pairs, axis=1)
    return table_times(table_y, rows).reshape(PEERS, 16, rows.shape[1])


def forward_kernel(own_blocks, shared, alone, table_z, table_y, out, blocks):
    core = lax.axis_index("pool")
    unfold(shared, 256 * core, blocks, 0)
    unfold(alone, 0, blocks, 1)
    unfold(shared, 256 * (1 - core), blocks, 2)
    read = reader(own_blocks, blocks)

    def density(unit, half, plane):
        left, right = places(unit)
        left, right = read(left, plane), turned(unit, half, read(right, plane))
        if unit == EIGHT and half:
            own = read(0, plane)
            left, right = jnp.where(on_eight(), own, left), jnp.where(on_eight(), own, right)
        return left * right

    for u in range(UNITS):
        rows = spectrum(
            [
                jnp.concatenate([density(u, 0, plane), density(u, 1, plane)], axis=1)
                for plane in range(4)
            ],
            table_z,
            table_y,
        )
        for ky_high in range(2):
            for high in range(2):
                at = 32 * u + 16 * ky_high + 8 * high
                out[:, at : at + 8, :] = rows[
                    :, 8 * ky_high : 8 * ky_high + 8, LANES * high : LANES * high + LANES
                ]

    last = []
    for at, behind in ((own_blocks[0], own_blocks[2]), (own_blocks[1], own_blocks[3])):
        pairs = jnp.where(low_lanes(N), at * swap(at), behind * swap(behind))
        last.append(jnp.concatenate([pairs, jnp.zeros((N, LANES), jnp.float32)], axis=1))
    rows = spectrum(last, table_z, table_y)
    out[:, 32 * UNITS :, :] = jnp.where(on_first(), rows[:, :8], rows[:, 8:])


def middle_kernel(spectra, kernel, table_x, table_x_back, out):
    low = low_lanes(N)
    first, second = (kernel[:, at : at + LANES] * (-1.0 / CELLS) for at in (0, LANES))

    def twice(value):
        other = swap(value)
        return jnp.where(low, value, other), jnp.where(low, other, value)

    def rows_of(pair):
        return jnp.concatenate([*pair, *pair], axis=0)

    def apply(rows, coulomb):
        return table_times(table_x_back, table_times(table_x, rows) * coulomb)

    coulombs = jnp.concatenate([rows_of(twice(first)), rows_of(twice(second))], axis=1)
    for u in range(UNITS):
        starts = 32 * u, 32 * u + 16
        rows = jnp.concatenate(
            [spectra[:, at : at + 16, :].reshape(256, LANES) for at in starts], axis=1
        )
        rows = apply(rows, coulombs)
        for part, at in enumerate(starts):
            out[:, at : at + 16, :] = rows[:, part * LANES : part * LANES + LANES].reshape(
                PEERS, 16, LANES
            )

    at = 32 * UNITS
    rows = spectra[:, at:, :]
    rows = jnp.concatenate([rows, pltpu.roll(rows, N, 2)], axis=1).reshape(256, LANES)
    mine = jnp.where(on_first(), first, second)
    rows = apply(rows, rows_of((mine, swap(mine)))).reshape(PEERS, 16, LANES)
    behind = pltpu.roll(rows[:, 8:], N, 2)
    front = lax.broadcasted_iota(jnp.int32, behind.shape, 2) < N
    out[:, at:, :] = jnp.where(front, rows[:, :8], behind)


def backward_kernel(
    returned,
    own_blocks,
    blocks,
    table_y_back,
    table_z_back,
    own_field,
    shared_field,
    lone_field,
    other_field,
    fields,
):
    fields[...] = jnp.zeros_like(fields)
    read = reader(own_blocks, blocks)

    def collect(unit, half, plane, potential):
        left, right = places(unit)
        partner = turned(unit, half, read(right, plane))
        given = turned(unit, half, potential * read(left, plane))
        if unit == EIGHT and half:
            squares = jnp.where(on_eight(), potential, 0.0)
            potential = potential - squares
            given = jnp.where(on_eight(), 0.0, given)
            fields[plane] += squares * read(0, plane)
        fields[4 * left + plane] += potential * partner
        fields[4 * right + plane] += given

    def potentials(pairs):
        rows = table_times(table_y_back, jnp.concatenate(pairs, axis=1))
        planes_of = [
            jnp.concatenate(
                [
                    rows[
                        at * LANES + part * N : at * LANES + part * N + N,
                        high * LANES : high * LANES + LANES,
                    ]
                    for part in range(2)
                ],
                axis=1,
            )
            for high in range(len(pairs))
            for at in range(2)
        ]
        return times_table(jnp.concatenate(planes_of, axis=0), table_z_back)

    for u in range(UNITS):
        pairs = []
        for high in range(2):
            at = 32 * u + 8 * high
            both = [returned[:, at : at + 8, :], returned[:, at + 16 : at + 24, :]]
            pairs.append(jnp.concatenate(both, axis=1).reshape(256, LANES))
        rows = potentials(pairs)
        for plane in range(4):
            for half in range(2):
                collect(
                    u,
                    half,
                    plane,
                    rows[plane * N : plane * N + N, half * LANES : half * LANES + LANES],
                )
    last = returned[:, 32 * UNITS :, :]
    last = [jnp.where(on_first(), last, 0.0), jnp.where(on_first(), 0.0, last)]
    rows = potentials([jnp.concatenate(last, axis=1).reshape(256, LANES)])
    low = low_lanes(N)
    for at in range(2):
        potential = rows[at * N : at * N + N, :LANES]
        other = swap(potential)
        fields[at] += jnp.where(low, potential, other) * swap(own_blocks[at])
        fields[2 + at] += jnp.where(low, other, potential) * swap(own_blocks[2 + at])
    for place, field in enumerate((own_field, shared_field, lone_field, other_field)):
        field[...] = fields[4 * place : 4 * place + 4]


def share_kernel(mine, others, relayed, field):
    at = 4 * (1 - lax.axis_index("pool"))
    for plane in range(4):
        field[plane] = mine[plane] + others[at + plane] + relayed[plane]


def final_kernel(both, out):
    low = low_lanes(HALF)
    for plane in range(4):
        even, odd = (
            both[plane, at : at + HALF] + both[4 + plane, at : at + HALF] for at in (0, HALF)
        )
        out[pl.ds(plane, HALF, stride=4), :] = jnp.where(low, even, swap(odd))
        out[pl.ds(128 + plane, HALF, stride=4), :] = jnp.where(low, swap(even), odd)


VMEM = pl.BlockSpec(memory_space=pltpu.VMEM)
PARAMS = pltpu.CompilerParams(vmem_limit_bytes=32 * 1024 * 1024)
CHUNKS = jax.ShapeDtypeStruct((PEERS, ROWS, LANES), jnp.float32)


def planes(count):
    return jax.ShapeDtypeStruct((count, N, LANES), jnp.float32)


LONG = pl.CostEstimate(flops=10**10, bytes_accessed=10**6, transcendentals=0)


def first(own):
    return pl.pallas_call(
        first_kernel,
        out_shape=[planes(4), jax.ShapeDtypeStruct((256, LANES), jnp.float32)],
        in_specs=[VMEM],
        out_specs=[VMEM] * 2,
        compiler_params=PARAMS,
        cost_estimate=LONG,
    )(own)


def forward(own_blocks, shared, alone, table_z, table_y):
    return pl.pallas_call(
        forward_kernel,
        out_shape=[CHUNKS, planes(12)],
        in_specs=[VMEM] * 5,
        out_specs=[VMEM] * 2,
        compiler_params=PARAMS,
    )(own_blocks, shared, alone, table_z, table_y)


def middle(spectra, kernel, table_x, table_x_back):
    return pl.pallas_call(
        middle_kernel,
        out_shape=CHUNKS,
        in_specs=[VMEM] * 4,
        out_specs=VMEM,
        compiler_params=PARAMS,
    )(spectra, kernel, table_x, table_x_back)


def backward(returned, own_blocks, blocks, table_y_back, table_z_back):
    return pl.pallas_call(
        backward_kernel,
        out_shape=[planes(4)] * 4,
        in_specs=[VMEM] * 5,
        out_specs=[VMEM] * 4,
        scratch_shapes=[pltpu.VMEM((16, N, LANES), jnp.float32)],
        compiler_params=PARAMS,
    )(returned, own_blocks, blocks, table_y_back, table_z_back)


def share(mine, others, relayed):
    return pl.pallas_call(
        share_kernel,
        out_shape=planes(4),
        in_specs=[VMEM] * 3,
        out_specs=VMEM,
        compiler_params=PARAMS,
    )(mine, others, relayed)


def final(both):
    return pl.pallas_call(
        final_kernel,
        out_shape=jax.ShapeDtypeStruct((256, LANES), jnp.float32),
        in_specs=[VMEM],
        out_specs=VMEM,
        compiler_params=PARAMS,
    )(both)


def along_band(value, steps):
    count = lax.axis_size("band")
    pairs = [
        (2 * source + core, 2 * ((source + steps[core]) % count) + core)
        for source in range(count)
        for core in range(2)
    ]
    return lax.ppermute(value, ("band", "pool"), pairs)


def both_cores(value):
    return lax.all_gather(value, "pool", tiled=True)


def exchange(value):
    return lax.all_to_all(value, "fft", split_axis=0, concat_axis=0, tiled=True)


def local(orbitals, kernel):
    table_z, table_y, table_x, table_x_back, table_y_back, table_z_back = [
        jnp.asarray(t) for t in tables()
    ]
    own = orbitals.reshape(2, 4, HALF, LANES).transpose(0, 2, 1, 3).reshape(256, LANES)
    shared = both_cores(along_band(own, [-s for s in SHARED]))
    own_blocks, own_again = first(own)
    alone = along_band(own_again, [-s for s in ALONE])
    spectra, blocks = forward(own_blocks, shared, alone, table_z, table_y)
    returned = exchange(middle(exchange(spectra), kernel, table_x, table_x_back))
    own_field, shared_field, lone_field, other_field = backward(
        returned, own_blocks, blocks, table_y_back, table_z_back
    )
    relayed = along_band(lone_field, RELAY)
    shared_field = along_band(share(shared_field, both_cores(other_field), relayed), SHARED)
    field = final(both_cores(shared_field + own_field))
    return field.reshape(2, HALF, 4, LANES).transpose(0, 2, 1, 3).reshape(2, 4, N * N)


def solution(mesh):
    return jax.shard_map(
        local,
        mesh=mesh,
        in_specs=(P("band", "fft", None), P(None, "fft")),
        out_specs=P("band", "fft", None),
        check_vma=False,
    )
```

```python
import jax
import jax.numpy as jnp
import ml_dtypes
import numpy as np
from jax import lax
from jax.experimental import pallas as pl
from jax.experimental.pallas import tpu as pltpu
from jax.sharding import PartitionSpec as P

N = 64
HALF = N // 2
CELLS = N * N * N
LANES = 2 * N
PEERS = 16
UNITS = 4
ROWS = 32 * UNITS + 8

SHARED = (-3, 4)
ALONE = (-2, 5)
RELAY = tuple(lone - shared for lone, shared in zip(ALONE, SHARED))
MEETINGS = (((0, 2), (0, 2)), ((0, 1), (0, 1)), ((1, 2), (1, 3)), ((2, 3), (2, 3)))
EIGHT = 3
EIGHT_CORE = 1
SOON = 1


def wave_parts(rows, columns):
    angle = 2.0 * np.pi / N * ((rows * columns) % N)
    return np.cos(angle), np.sin(angle)


def split_table(table):
    high = table.astype(ml_dtypes.bfloat16)
    low = (table - high.astype(np.float64)).astype(ml_dtypes.bfloat16)
    return np.stack([high, low])


def tables():
    index = np.arange(N)
    cosine, sine = wave_parts(index[:, None], index[None, :])
    turn = np.stack([np.stack([cosine, sine]), np.stack([-sine, cosine])])
    two = np.eye(2)
    along_z = np.einsum("oikz,ab->iazobk", turn, two).reshape(256, 256)
    along_y = np.einsum("oiky,ab->kaoiby", turn, two)
    along_y = along_y.reshape(PEERS, 2, 2, 2, 2, 2, 2, HALF, 2)
    along_y = along_y.transpose(0, 1, 4, 3, 2, 6, 5, 8, 7).reshape(256, 256)
    along_x = np.einsum("oikx,ab->oakxib", turn, two).reshape(2, 2, N, HALF, 2, 2, 2)
    along_x = along_x.transpose(0, 1, 2, 3, 5, 4, 6).reshape(256, 256)
    return [split_table(t) for t in (along_z, along_y, along_x, along_x.T, along_y.T, along_z.T)]


def halves(value):
    high = value.astype(jnp.bfloat16)
    low = (value - high.astype(jnp.float32)).astype(jnp.bfloat16)
    return high, low


def dot(left, right):
    return jnp.dot(left, right, preferred_element_type=jnp.float32)


def times_table(value, table):
    high, low = halves(value)
    return dot(high, table[0]) + dot(low, table[0]) + dot(high, table[1])


def table_times(table, value):
    high, low = halves(value)
    return dot(table[0], high) + dot(table[0], low) + dot(table[1], high)


def swap(value):
    return pltpu.roll(value, N, 1)


def low_lanes(rows):
    return lax.broadcasted_iota(jnp.int32, (rows, LANES), 1) < N


def on_first():
    return lax.axis_index("pool") == 0


def on_eight():
    return lax.axis_index("pool") == EIGHT_CORE


def pick(first, second):
    return first if first == second else jnp.where(on_first(), first, second)


def places(unit):
    first, second = MEETINGS[unit]
    return (first[0], second[0]), (first[1], second[1])


def turned(unit, half, value):
    if unit == EIGHT and not half:
        return jnp.where(on_eight() & (lax.axis_index("band") >= 8), swap(value), value)
    return swap(value) if half else value


def reader(own_blocks, shared_blocks, lone_blocks):
    def read_one(place, plane):
        if place == 0:
            return own_blocks[plane]
        if place == 2:
            return lone_blocks[plane]
        return shared_blocks[2 * place - 2 + plane]

    def read(of_cores, plane):
        first, second = of_cores
        if first == second:
            return read_one(first, plane)
        return jnp.where(on_first(), read_one(first, plane), read_one(second, plane))

    return read


def unfold(source, base, blocks, place):
    low = low_lanes(HALF)
    for plane in range(4):
        first = source[pl.ds(base + plane, HALF, stride=4), :]
        second = source[pl.ds(base + 128 + plane, HALF, stride=4), :]
        blocks[4 * place + plane, :HALF] = jnp.where(low, first, swap(second))
        blocks[4 * place + plane, HALF:] = jnp.where(low, swap(first), second)


def first_kernel(own, blocks, again):
    unfold(own, 0, blocks, 0)
    again[...] = own[...]


def spectrum(density, table_z, table_y):
    rows = times_table(jnp.concatenate(density, axis=0), table_z)
    pairs = [
        jnp.concatenate(
            [
                rows[base + at * N : base + at * N + N, part * LANES : part * LANES + LANES]
                for at in range(2)
                for part in range(2)
            ],
            axis=0,
        )
        for base in range(0, rows.shape[0], LANES)
    ]
    rows = jnp.concatenate(pairs, axis=1)
    return table_times(table_y, rows).reshape(PEERS, 16, rows.shape[1])


def density(read, unit, half, plane):
    left, right = places(unit)
    left, right = read(left, plane), turned(unit, half, read(right, plane))
    if unit == EIGHT and half:
        own = read((0, 0), plane)
        left, right = jnp.where(on_eight(), own, left), jnp.where(on_eight(), own, right)
    return left * right


def send_unit(read, unit, out, base, table_z, table_y):
    rows = spectrum(
        [
            jnp.concatenate([density(read, unit, half, plane) for half in range(2)], axis=1)
            for plane in range(4)
        ],
        table_z,
        table_y,
    )
    for ky_high in range(2):
        for high in range(2):
            at = base + 16 * ky_high + 8 * high
            out[:, at : at + 8, :] = rows[
                :, 8 * ky_high : 8 * ky_high + 8, LANES * high : LANES * high + LANES
            ]


def early_kernel(own_blocks, shared, table_z, table_y, out, shared_blocks):
    core = lax.axis_index("pool")
    unfold(shared, 256 * core, shared_blocks, 0)
    unfold(shared, 256 * (1 - core), shared_blocks, 1)
    read = reader(own_blocks, shared_blocks, None)
    send_unit(read, SOON, out, 0, table_z, table_y)
    last = []
    for at, behind in ((own_blocks[0], own_blocks[2]), (own_blocks[1], own_blocks[3])):
        pairs = jnp.where(low_lanes(N), at * swap(at), behind * swap(behind))
        last.append(jnp.concatenate([pairs, jnp.zeros((N, LANES), jnp.float32)], axis=1))
    rows = spectrum(last, table_z, table_y)
    out[:, 32:, :] = jnp.where(on_first(), rows[:, :8], rows[:, 8:])


def forward_kernel(own_blocks, shared_blocks, early, alone, table_z, table_y, out, lone_blocks):
    out[:, 32 * SOON : 32 * SOON + 32, :] = early[:, :32, :]
    out[:, 32 * UNITS :, :] = early[:, 32:, :]
    unfold(alone, 0, lone_blocks, 0)
    read = reader(own_blocks, shared_blocks, lone_blocks)
    for u in range(UNITS):
        if u != SOON:
            send_unit(read, u, out, 32 * u, table_z, table_y)


def middle_kernel(spectra, kernel, table_x, table_x_back, out):
    low = low_lanes(N)
    first, second = (kernel[:, at : at + LANES] * (-1.0 / CELLS) for at in (0, LANES))

    def twice(value):
        other = swap(value)
        return jnp.where(low, value, other), jnp.where(low, other, value)

    def rows_of(pair):
        return jnp.concatenate([*pair, *pair], axis=0)

    def apply(rows, coulomb):
        return table_times(table_x_back, table_times(table_x, rows) * coulomb)

    coulombs = jnp.concatenate([rows_of(twice(first)), rows_of(twice(second))], axis=1)
    for u in range(UNITS):
        starts = 32 * u, 32 * u + 16
        rows = jnp.concatenate(
            [spectra[:, at : at + 16, :].reshape(256, LANES) for at in starts], axis=1
        )
        rows = apply(rows, coulombs)
        for part, at in enumerate(starts):
            out[:, at : at + 16, :] = rows[:, part * LANES : part * LANES + LANES].reshape(
                PEERS, 16, LANES
            )

    at = 32 * UNITS
    rows = spectra[:, at:, :]
    rows = jnp.concatenate([rows, pltpu.roll(rows, N, 2)], axis=1).reshape(256, LANES)
    mine = jnp.where(on_first(), first, second)
    rows = apply(rows, rows_of((mine, swap(mine)))).reshape(PEERS, 16, LANES)
    behind = pltpu.roll(rows[:, 8:], N, 2)
    front = lax.broadcasted_iota(jnp.int32, behind.shape, 2) < N
    out[:, at:, :] = jnp.where(front, rows[:, :8], behind)


def backward_kernel(
    returned,
    own_blocks,
    shared_blocks,
    lone_blocks,
    table_y_back,
    table_z_back,
    own_field,
    shared_field,
    lone_field,
    other_field,
    fields,
):
    fields[...] = jnp.zeros_like(fields)
    read = reader(own_blocks, shared_blocks, lone_blocks)

    def collect(unit, half, plane, potential):
        left, right = places(unit)
        partner = turned(unit, half, read(right, plane))
        given = turned(unit, half, potential * read(left, plane))
        if unit == EIGHT and half:
            squares = jnp.where(on_eight(), potential, 0.0)
            potential = potential - squares
            given = jnp.where(on_eight(), 0.0, given)
            fields[plane] += squares * own_blocks[plane]
        fields[4 * pick(*left) + plane] += potential * partner
        fields[4 * pick(*right) + plane] += given

    def potentials(pairs):
        rows = table_times(table_y_back, jnp.concatenate(pairs, axis=1))
        planes_of = [
            jnp.concatenate(
                [
                    rows[
                        at * LANES + part * N : at * LANES + part * N + N,
                        high * LANES : high * LANES + LANES,
                    ]
                    for part in range(2)
                ],
                axis=1,
            )
            for high in range(len(pairs))
            for at in range(2)
        ]
        return times_table(jnp.concatenate(planes_of, axis=0), table_z_back)

    for u in range(UNITS):
        pairs = []
        for high in range(2):
            at = 32 * u + 8 * high
            both = [returned[:, at : at + 8, :], returned[:, at + 16 : at + 24, :]]
            pairs.append(jnp.concatenate(both, axis=1).reshape(256, LANES))
        rows = potentials(pairs)
        for plane in range(4):
            for half in range(2):
                collect(
                    u,
                    half,
                    plane,
                    rows[plane * N : plane * N + N, half * LANES : half * LANES + LANES],
                )
    last = returned[:, 32 * UNITS :, :]
    last = [jnp.where(on_first(), last, 0.0), jnp.where(on_first(), 0.0, last)]
    rows = potentials([jnp.concatenate(last, axis=1).reshape(256, LANES)])
    low = low_lanes(N)
    for at in range(2):
        potential = rows[at * N : at * N + N, :LANES]
        other = swap(potential)
        fields[at] += jnp.where(low, potential, other) * swap(own_blocks[at])
        fields[2 + at] += jnp.where(low, other, potential) * swap(own_blocks[2 + at])
    for place, field in enumerate((own_field, shared_field, lone_field, other_field)):
        field[...] = fields[4 * place : 4 * place + 4]


def share_kernel(mine, others, relayed, field):
    at = 4 * (1 - lax.axis_index("pool"))
    for plane in range(4):
        field[plane] = mine[plane] + others[at + plane] + relayed[plane]


def final_kernel(both, out):
    low = low_lanes(HALF)
    for plane in range(4):
        even, odd = (
            both[plane, at : at + HALF] + both[4 + plane, at : at + HALF] for at in (0, HALF)
        )
        out[pl.ds(plane, HALF, stride=4), :] = jnp.where(low, even, swap(odd))
        out[pl.ds(128 + plane, HALF, stride=4), :] = jnp.where(low, swap(even), odd)


VMEM = pl.BlockSpec(memory_space=pltpu.VMEM)
PARAMS = pltpu.CompilerParams(vmem_limit_bytes=32 * 1024 * 1024)
CHUNKS = jax.ShapeDtypeStruct((PEERS, ROWS, LANES), jnp.float32)


def planes(count):
    return jax.ShapeDtypeStruct((count, N, LANES), jnp.float32)


LONG = pl.CostEstimate(flops=10**10, bytes_accessed=10**6, transcendentals=0)


def first(own):
    return pl.pallas_call(
        first_kernel,
        out_shape=[planes(4), jax.ShapeDtypeStruct((256, LANES), jnp.float32)],
        in_specs=[VMEM],
        out_specs=[VMEM] * 2,
        compiler_params=PARAMS,
        cost_estimate=LONG,
    )(own)


def early(own_blocks, shared, table_z, table_y):
    return pl.pallas_call(
        early_kernel,
        out_shape=[jax.ShapeDtypeStruct((PEERS, 40, LANES), jnp.float32), planes(8)],
        in_specs=[VMEM] * 4,
        out_specs=[VMEM] * 2,
        compiler_params=PARAMS,
    )(own_blocks, shared, table_z, table_y)


def forward(own_blocks, shared_blocks, rows, alone, table_z, table_y):
    return pl.pallas_call(
        forward_kernel,
        out_shape=[CHUNKS, planes(4)],
        in_specs=[VMEM] * 6,
        out_specs=[VMEM] * 2,
        compiler_params=PARAMS,
    )(own_blocks, shared_blocks, rows, alone, table_z, table_y)


def middle(spectra, kernel, table_x, table_x_back):
    return pl.pallas_call(
        middle_kernel,
        out_shape=CHUNKS,
        in_specs=[VMEM] * 4,
        out_specs=VMEM,
        compiler_params=PARAMS,
    )(spectra, kernel, table_x, table_x_back)


def backward(returned, own_blocks, shared_blocks, lone_blocks, table_y_back, table_z_back):
    return pl.pallas_call(
        backward_kernel,
        out_shape=[planes(4)] * 4,
        in_specs=[VMEM] * 6,
        out_specs=[VMEM] * 4,
        scratch_shapes=[pltpu.VMEM((16, N, LANES), jnp.float32)],
        compiler_params=PARAMS,
    )(returned, own_blocks, shared_blocks, lone_blocks, table_y_back, table_z_back)


def share(mine, others, relayed):
    return pl.pallas_call(
        share_kernel,
        out_shape=planes(4),
        in_specs=[VMEM] * 3,
        out_specs=VMEM,
        compiler_params=PARAMS,
    )(mine, others, relayed)


def final(both):
    return pl.pallas_call(
        final_kernel,
        out_shape=jax.ShapeDtypeStruct((256, LANES), jnp.float32),
        in_specs=[VMEM],
        out_specs=VMEM,
        compiler_params=PARAMS,
    )(both)


def along_band(value, steps):
    count = lax.axis_size("band")
    pairs = [
        (2 * source + core, 2 * ((source + steps[core]) % count) + core)
        for source in range(count)
        for core in range(2)
    ]
    return lax.ppermute(value, ("band", "pool"), pairs)


def both_cores(value):
    return lax.all_gather(value, "pool", tiled=True)


def exchange(value):
    return lax.all_to_all(value, "fft", split_axis=0, concat_axis=0, tiled=True)


def local(orbitals, kernel):
    table_z, table_y, table_x, table_x_back, table_y_back, table_z_back = [
        jnp.asarray(t) for t in tables()
    ]
    own = orbitals.reshape(2, 4, HALF, LANES).transpose(0, 2, 1, 3).reshape(256, LANES)
    shared = both_cores(along_band(own, [-s for s in SHARED]))
    own_blocks, own_again = first(own)
    alone = along_band(own_again, [-s for s in ALONE])
    rows, shared_blocks = early(own_blocks, shared, table_z, table_y)
    spectra, lone_blocks = forward(own_blocks, shared_blocks, rows, alone, table_z, table_y)
    returned = exchange(middle(exchange(spectra), kernel, table_x, table_x_back))
    own_field, shared_field, lone_field, other_field = backward(
        returned, own_blocks, shared_blocks, lone_blocks, table_y_back, table_z_back
    )
    relayed = along_band(lone_field, RELAY)
    shared_field = along_band(share(shared_field, both_cores(other_field), relayed), SHARED)
    field = final(both_cores(shared_field + own_field))
    return field.reshape(2, HALF, 4, LANES).transpose(0, 2, 1, 3).reshape(2, 4, N * N)


def solution(mesh):
    return jax.shard_map(
        local,
        mesh=mesh,
        in_specs=(P("band", "fft", None), P(None, "fft")),
        out_specs=P("band", "fft", None),
        check_vma=False,
    )
```

```python
import jax
import jax.numpy as jnp
import ml_dtypes
import numpy as np
from jax import lax
from jax.experimental import pallas as pl
from jax.experimental.pallas import tpu as pltpu
from jax.sharding import PartitionSpec as P

N = 64
HALF = N // 2
CELLS = N * N * N
LANES = 2 * N
PEERS = 16
UNITS = 4
ROWS = 32 * UNITS + 8

SHARED = (-3, 4)
ALONE = (5, -2)
RELAY = (1, 1)
MEETINGS = (((0, 2), (0, 2)), ((0, 1), (0, 1)), ((1, 3), (2, 3)), ((1, 2), (1, 2)))
EIGHT = 3
EIGHT_CORE = 0


def wave_parts(rows, columns):
    angle = 2.0 * np.pi / N * ((rows * columns) % N)
    return np.cos(angle), np.sin(angle)


def split_table(table):
    high = table.astype(ml_dtypes.bfloat16)
    low = (table - high.astype(np.float64)).astype(ml_dtypes.bfloat16)
    return np.stack([high, low])


def tables():
    index = np.arange(N)
    cosine, sine = wave_parts(index[:, None], index[None, :])
    turn = np.stack([np.stack([cosine, sine]), np.stack([-sine, cosine])])
    two = np.eye(2)
    along_z = np.einsum("oikz,ab->iazobk", turn, two).reshape(256, 256)
    along_y = np.einsum("oiky,ab->kaoiby", turn, two)
    along_y = along_y.reshape(PEERS, 2, 2, 2, 2, 2, 2, HALF, 2)
    along_y = along_y.transpose(0, 1, 4, 3, 2, 6, 5, 8, 7).reshape(256, 256)
    along_x = np.einsum("oikx,ab->oakxib", turn, two).reshape(2, 2, N, HALF, 2, 2, 2)
    along_x = along_x.transpose(0, 1, 2, 3, 5, 4, 6).reshape(256, 256)
    return [split_table(t) for t in (along_z, along_y, along_x, along_x.T, along_y.T, along_z.T)]


def halves(value):
    high = value.astype(jnp.bfloat16)
    low = (value - high.astype(jnp.float32)).astype(jnp.bfloat16)
    return high, low


def dot(left, right):
    return jnp.dot(left, right, preferred_element_type=jnp.float32)


def times_table(value, table):
    high, low = halves(value)
    return dot(high, table[0]) + dot(low, table[0]) + dot(high, table[1])


def table_times(table, value):
    high, low = halves(value)
    return dot(table[0], high) + dot(table[0], low) + dot(table[1], high)


def swap(value):
    return pltpu.roll(value, N, 1)


def low_lanes(rows):
    return lax.broadcasted_iota(jnp.int32, (rows, LANES), 1) < N


def on_first():
    return lax.axis_index("pool") == 0


def on_eight():
    return lax.axis_index("pool") == EIGHT_CORE


def pick(first, second):
    return first if first is second else jnp.where(on_first(), first, second)


def places(unit):
    first, second = MEETINGS[unit]
    return pick(first[0], second[0]), pick(first[1], second[1])


def turned(unit, half, value):
    if unit == EIGHT and not half:
        return jnp.where(on_eight() & (lax.axis_index("band") >= 8), swap(value), value)
    return swap(value) if half else value


def reader(own_blocks, blocks):
    def read(place, plane):
        if isinstance(place, int):
            return blocks[4 * place - 4 + plane] if place else own_blocks[plane]
        return blocks[4 * place - 4 + plane]

    return read


def unfold(source, base, blocks, place):
    low = low_lanes(HALF)
    for plane in range(4):
        first = source[pl.ds(base + plane, HALF, stride=4), :]
        second = source[pl.ds(base + 128 + plane, HALF, stride=4), :]
        blocks[4 * place + plane, :HALF] = jnp.where(low, first, swap(second))
        blocks[4 * place + plane, HALF:] = jnp.where(low, swap(first), second)


def first_kernel(own, blocks, again):
    unfold(own, 0, blocks, 0)
    again[...] = own[...]


def spectrum(density, table_z, table_y):
    rows = times_table(jnp.concatenate(density, axis=0), table_z)
    pairs = [
        jnp.concatenate(
            [
                rows[base + at * N : base + at * N + N, part * LANES : part * LANES + LANES]
                for at in range(2)
                for part in range(2)
            ],
            axis=0,
        )
        for base in range(0, rows.shape[0], LANES)
    ]
    rows = jnp.concatenate(pairs, axis=1)
    return table_times(table_y, rows).reshape(PEERS, 16, rows.shape[1])


def forward_kernel(own_blocks, shared, alone, table_z, table_y, out, blocks):
    core = lax.axis_index("pool")
    unfold(shared, 256 * core, blocks, 0)
    unfold(alone, 0, blocks, 1)
    unfold(shared, 256 * (1 - core), blocks, 2)
    read = reader(own_blocks, blocks)

    def density(unit, half, plane):
        left, right = places(unit)
        left, right = read(left, plane), turned(unit, half, read(right, plane))
        if unit == EIGHT and half:
            own = read(0, plane)
            left, right = jnp.where(on_eight(), own, left), jnp.where(on_eight(), own, right)
        return left * right

    for u in range(UNITS):
        rows = spectrum(
            [
                jnp.concatenate([density(u, 0, plane), density(u, 1, plane)], axis=1)
                for plane in range(4)
            ],
            table_z,
            table_y,
        )
        for ky_high in range(2):
            for high in range(2):
                at = 32 * u + 16 * ky_high + 8 * high
                out[:, at : at + 8, :] = rows[
                    :, 8 * ky_high : 8 * ky_high + 8, LANES * high : LANES * high + LANES
                ]

    last = []
    for at, behind in ((own_blocks[0], own_blocks[2]), (own_blocks[1], own_blocks[3])):
        pairs = jnp.where(low_lanes(N), at * swap(at), behind * swap(behind))
        last.append(jnp.concatenate([pairs, jnp.zeros((N, LANES), jnp.float32)], axis=1))
    rows = spectrum(last, table_z, table_y)
    out[:, 32 * UNITS :, :] = jnp.where(on_first(), rows[:, :8], rows[:, 8:])


def middle_kernel(spectra, kernel, table_x, table_x_back, out):
    low = low_lanes(N)
    first, second = (kernel[:, at : at + LANES] * (-1.0 / CELLS) for at in (0, LANES))

    def twice(value):
        other = swap(value)
        return jnp.where(low, value, other), jnp.where(low, other, value)

    def rows_of(pair):
        return jnp.concatenate([*pair, *pair], axis=0)

    def apply(rows, coulomb):
        return table_times(table_x_back, table_times(table_x, rows) * coulomb)

    coulombs = jnp.concatenate([rows_of(twice(first)), rows_of(twice(second))], axis=1)
    for u in range(UNITS):
        starts = 32 * u, 32 * u + 16
        rows = jnp.concatenate(
            [spectra[:, at : at + 16, :].reshape(256, LANES) for at in starts], axis=1
        )
        rows = apply(rows, coulombs)
        for part, at in enumerate(starts):
            out[:, at : at + 16, :] = rows[:, part * LANES : part * LANES + LANES].reshape(
                PEERS, 16, LANES
            )

    at = 32 * UNITS
    rows = spectra[:, at:, :]
    rows = jnp.concatenate([rows, pltpu.roll(rows, N, 2)], axis=1).reshape(256, LANES)
    mine = jnp.where(on_first(), first, second)
    rows = apply(rows, rows_of((mine, swap(mine)))).reshape(PEERS, 16, LANES)
    behind = pltpu.roll(rows[:, 8:], N, 2)
    front = lax.broadcasted_iota(jnp.int32, behind.shape, 2) < N
    out[:, at:, :] = jnp.where(front, rows[:, :8], behind)


def backward_kernel(
    returned,
    own_blocks,
    blocks,
    table_y_back,
    table_z_back,
    own_field,
    shared_field,
    lone_field,
    other_field,
    fields,
):
    fields[...] = jnp.zeros_like(fields)
    read = reader(own_blocks, blocks)

    def collect(unit, half, plane, potential):
        left, right = places(unit)
        partner = turned(unit, half, read(right, plane))
        given = turned(unit, half, potential * read(left, plane))
        if unit == EIGHT and half:
            squares = jnp.where(on_eight(), potential, 0.0)
            potential = potential - squares
            given = jnp.where(on_eight(), 0.0, given)
            fields[plane] += squares * read(0, plane)
        fields[4 * left + plane] += potential * partner
        fields[4 * right + plane] += given

    def potentials(pairs):
        rows = table_times(table_y_back, jnp.concatenate(pairs, axis=1))
        planes_of = [
            jnp.concatenate(
                [
                    rows[
                        at * LANES + part * N : at * LANES + part * N + N,
                        high * LANES : high * LANES + LANES,
                    ]
                    for part in range(2)
                ],
                axis=1,
            )
            for high in range(len(pairs))
            for at in range(2)
        ]
        return times_table(jnp.concatenate(planes_of, axis=0), table_z_back)

    for u in range(UNITS):
        pairs = []
        for high in range(2):
            at = 32 * u + 8 * high
            both = [returned[:, at : at + 8, :], returned[:, at + 16 : at + 24, :]]
            pairs.append(jnp.concatenate(both, axis=1).reshape(256, LANES))
        rows = potentials(pairs)
        for plane in range(4):
            for half in range(2):
                collect(
                    u,
                    half,
                    plane,
                    rows[plane * N : plane * N + N, half * LANES : half * LANES + LANES],
                )
    last = returned[:, 32 * UNITS :, :]
    last = [jnp.where(on_first(), last, 0.0), jnp.where(on_first(), 0.0, last)]
    rows = potentials([jnp.concatenate(last, axis=1).reshape(256, LANES)])
    low = low_lanes(N)
    for at in range(2):
        potential = rows[at * N : at * N + N, :LANES]
        other = swap(potential)
        fields[at] += jnp.where(low, potential, other) * swap(own_blocks[at])
        fields[2 + at] += jnp.where(low, other, potential) * swap(own_blocks[2 + at])
    for place, field in enumerate((own_field, shared_field, lone_field, other_field)):
        field[...] = fields[4 * place : 4 * place + 4]


def share_kernel(mine, others, relayed, field):
    at = 4 * (1 - lax.axis_index("pool"))
    for plane in range(4):
        field[plane] = mine[plane] + others[at + plane] + relayed[plane]


def final_kernel(both, out):
    low = low_lanes(HALF)
    for plane in range(4):
        even, odd = (
            both[plane, at : at + HALF] + both[4 + plane, at : at + HALF] for at in (0, HALF)
        )
        out[pl.ds(plane, HALF, stride=4), :] = jnp.where(low, even, swap(odd))
        out[pl.ds(128 + plane, HALF, stride=4), :] = jnp.where(low, swap(even), odd)


VMEM = pl.BlockSpec(memory_space=pltpu.VMEM)
PARAMS = pltpu.CompilerParams(vmem_limit_bytes=32 * 1024 * 1024)
CHUNKS = jax.ShapeDtypeStruct((PEERS, ROWS, LANES), jnp.float32)


def planes(count):
    return jax.ShapeDtypeStruct((count, N, LANES), jnp.float32)


LONG = pl.CostEstimate(flops=10**10, bytes_accessed=10**6, transcendentals=0)


def first(own):
    return pl.pallas_call(
        first_kernel,
        out_shape=[planes(4), jax.ShapeDtypeStruct((256, LANES), jnp.float32)],
        in_specs=[VMEM],
        out_specs=[VMEM] * 2,
        compiler_params=PARAMS,
        cost_estimate=LONG,
    )(own)


def forward(own_blocks, shared, alone, table_z, table_y):
    return pl.pallas_call(
        forward_kernel,
        out_shape=[CHUNKS, planes(12)],
        in_specs=[VMEM] * 5,
        out_specs=[VMEM] * 2,
        compiler_params=PARAMS,
    )(own_blocks, shared, alone, table_z, table_y)


def middle(spectra, kernel, table_x, table_x_back):
    return pl.pallas_call(
        middle_kernel,
        out_shape=CHUNKS,
        in_specs=[VMEM] * 4,
        out_specs=VMEM,
        compiler_params=PARAMS,
    )(spectra, kernel, table_x, table_x_back)


def backward(returned, own_blocks, blocks, table_y_back, table_z_back):
    return pl.pallas_call(
        backward_kernel,
        out_shape=[planes(4)] * 4,
        in_specs=[VMEM] * 5,
        out_specs=[VMEM] * 4,
        scratch_shapes=[pltpu.VMEM((16, N, LANES), jnp.float32)],
        compiler_params=PARAMS,
    )(returned, own_blocks, blocks, table_y_back, table_z_back)


def share(mine, others, relayed):
    return pl.pallas_call(
        share_kernel,
        out_shape=planes(4),
        in_specs=[VMEM] * 3,
        out_specs=VMEM,
        compiler_params=PARAMS,
    )(mine, others, relayed)


def final(both):
    return pl.pallas_call(
        final_kernel,
        out_shape=jax.ShapeDtypeStruct((256, LANES), jnp.float32),
        in_specs=[VMEM],
        out_specs=VMEM,
        compiler_params=PARAMS,
    )(both)


def along_band(value, steps, crossed=False):
    count = lax.axis_size("band")
    pairs = [
        (2 * source + core, 2 * ((source + steps[core]) % count) + (core ^ crossed))
        for source in range(count)
        for core in range(2)
    ]
    return lax.ppermute(value, ("band", "pool"), pairs)


def both_cores(value):
    return lax.all_gather(value, "pool", tiled=True)


def exchange(value):
    return lax.all_to_all(value, "fft", split_axis=0, concat_axis=0, tiled=True)


def local(orbitals, kernel):
    table_z, table_y, table_x, table_x_back, table_y_back, table_z_back = [
        jnp.asarray(t) for t in tables()
    ]
    own = orbitals.reshape(2, 4, HALF, LANES).transpose(0, 2, 1, 3).reshape(256, LANES)
    shared = both_cores(along_band(own, [-s for s in SHARED]))
    own_blocks, own_again = first(own)
    alone = along_band(own_again, [-s for s in ALONE])
    spectra, blocks = forward(own_blocks, shared, alone, table_z, table_y)
    returned = exchange(middle(exchange(spectra), kernel, table_x, table_x_back))
    own_field, shared_field, lone_field, other_field = backward(
        returned, own_blocks, blocks, table_y_back, table_z_back
    )
    relayed = along_band(lone_field, RELAY, True)
    shared_field = along_band(share(shared_field, both_cores(other_field), relayed), SHARED)
    field = final(both_cores(shared_field + own_field))
    return field.reshape(2, HALF, 4, LANES).transpose(0, 2, 1, 3).reshape(2, 4, N * N)


def solution(mesh):
    return jax.shard_map(
        local,
        mesh=mesh,
        in_specs=(P("band", "fft", None), P(None, "fft")),
        out_specs=P("band", "fft", None),
        check_vma=False,
    )
```

```python
import jax
import jax.numpy as jnp
import ml_dtypes
import numpy as np
from jax import lax
from jax.experimental import pallas as pl
from jax.experimental.pallas import tpu as pltpu
from jax.sharding import PartitionSpec as P

N = 64
HALF = N // 2
CELLS = N * N * N
LANES = 2 * N
PEERS = 16
UNITS = 4
ROWS = 32 * UNITS + 8

SHARED = (-3, 4)
ALONE = (5, -2)
RELAY = (1, 1)
MEETINGS = (((0, 2), (0, 2)), ((0, 1), (0, 1)), ((1, 3), (2, 3)), ((1, 2), (1, 2)))
EIGHT = 3
EIGHT_CORE = 0


def wave_parts(rows, columns):
    angle = 2.0 * np.pi / N * ((rows * columns) % N)
    return np.cos(angle), np.sin(angle)


def split_table(table):
    high = table.astype(ml_dtypes.bfloat16)
    low = (table - high.astype(np.float64)).astype(ml_dtypes.bfloat16)
    return np.stack([high, low])


def tables():
    index = np.arange(N)
    cosine, sine = wave_parts(index[:, None], index[None, :])
    turn = np.stack([np.stack([cosine, sine]), np.stack([-sine, cosine])])
    two = np.eye(2)
    along_z = np.einsum("oikz,ab->iazobk", turn, two).reshape(256, 256)
    along_y = np.einsum("oiky,ab->kaoiby", turn, two)
    along_y = along_y.reshape(PEERS, 2, 2, 2, 2, 2, 2, HALF, 2)
    along_y = along_y.transpose(0, 1, 4, 3, 2, 6, 5, 8, 7).reshape(256, 256)
    along_x = np.einsum("oikx,ab->oakxib", turn, two).reshape(2, 2, N, HALF, 2, 2, 2)
    along_x = along_x.transpose(0, 1, 2, 3, 5, 4, 6).reshape(256, 256)
    return [split_table(t) for t in (along_z, along_y, along_x, along_x.T, along_y.T, along_z.T)]


def halves(value):
    high = value.astype(jnp.bfloat16)
    low = (value - high.astype(jnp.float32)).astype(jnp.bfloat16)
    return high, low


def dot(left, right):
    return jnp.dot(left, right, preferred_element_type=jnp.float32)


def times_table(value, table):
    high, low = halves(value)
    return dot(high, table[0]) + dot(low, table[0]) + dot(high, table[1])


def table_times(table, value):
    high, low = halves(value)
    return dot(table[0], high) + dot(table[0], low) + dot(table[1], high)


def swap(value):
    return pltpu.roll(value, N, 1)


def low_lanes(rows):
    return lax.broadcasted_iota(jnp.int32, (rows, LANES), 1) < N


def on_first():
    return lax.axis_index("pool") == 0


def on_eight():
    return lax.axis_index("pool") == EIGHT_CORE


def pick(first, second):
    return first if first is second else jnp.where(on_first(), first, second)


def places(unit):
    first, second = MEETINGS[unit]
    return pick(first[0], second[0]), pick(first[1], second[1])


def turned(unit, half, value):
    if unit == EIGHT and not half:
        return jnp.where(on_eight() & (lax.axis_index("band") >= 8), swap(value), value)
    return swap(value) if half else value


def reader(own_blocks, blocks):
    def read(place, plane):
        if isinstance(place, int):
            return blocks[4 * place - 4 + plane] if place else own_blocks[plane]
        return blocks[4 * place - 4 + plane]

    return read


def unfold(source, base, blocks, place):
    low = low_lanes(HALF)
    for plane in range(4):
        first = source[pl.ds(base + plane, HALF, stride=4), :]
        second = source[pl.ds(base + 128 + plane, HALF, stride=4), :]
        blocks[4 * place + plane, :HALF] = jnp.where(low, first, swap(second))
        blocks[4 * place + plane, HALF:] = jnp.where(low, swap(first), second)


def first_kernel(own, blocks, again):
    unfold(own, 0, blocks, 0)
    again[...] = own[...]


def spectrum(density, table_z, table_y):
    rows = times_table(jnp.concatenate(density, axis=0), table_z)
    pairs = [
        jnp.concatenate(
            [
                rows[base + at * N : base + at * N + N, part * LANES : part * LANES + LANES]
                for at in range(2)
                for part in range(2)
            ],
            axis=0,
        )
        for base in range(0, rows.shape[0], LANES)
    ]
    rows = jnp.concatenate(pairs, axis=1)
    return table_times(table_y, rows).reshape(PEERS, 16, rows.shape[1])


def forward_kernel(own_blocks, shared, alone, table_z, table_y, out, blocks):
    core = lax.axis_index("pool")
    unfold(shared, 256 * core, blocks, 0)
    unfold(alone, 0, blocks, 1)
    unfold(shared, 256 * (1 - core), blocks, 2)
    read = reader(own_blocks, blocks)

    def density(unit, half, plane):
        left, right = places(unit)
        left, right = read(left, plane), turned(unit, half, read(right, plane))
        if unit == EIGHT and half:
            own = read(0, plane)
            left, right = jnp.where(on_eight(), own, left), jnp.where(on_eight(), own, right)
        return left * right

    for u in range(UNITS):
        rows = spectrum(
            [
                jnp.concatenate([density(u, 0, plane), density(u, 1, plane)], axis=1)
                for plane in range(4)
            ],
            table_z,
            table_y,
        )
        for ky_high in range(2):
            for high in range(2):
                at = 32 * u + 16 * ky_high + 8 * high
                out[:, at : at + 8, :] = rows[
                    :, 8 * ky_high : 8 * ky_high + 8, LANES * high : LANES * high + LANES
                ]

    last = []
    for at, behind in ((own_blocks[0], own_blocks[2]), (own_blocks[1], own_blocks[3])):
        pairs = jnp.where(low_lanes(N), at * swap(at), behind * swap(behind))
        last.append(pairs)
    rows = spectrum(last, table_z[:, :LANES], table_y)
    out[:, 32 * UNITS :, :] = jnp.where(on_first(), rows[:, :8], rows[:, 8:])


def middle_kernel(spectra, kernel, table_x, table_x_back, out):
    low = low_lanes(N)
    first, second = (kernel[:, at : at + LANES] * (-1.0 / CELLS) for at in (0, LANES))

    def twice(value):
        other = swap(value)
        return jnp.where(low, value, other), jnp.where(low, other, value)

    def rows_of(pair):
        return jnp.concatenate([*pair, *pair], axis=0)

    def apply(rows, coulomb):
        return table_times(table_x_back, table_times(table_x, rows) * coulomb)

    coulombs = jnp.concatenate([rows_of(twice(first)), rows_of(twice(second))], axis=1)
    for u in range(UNITS):
        starts = 32 * u, 32 * u + 16
        rows = jnp.concatenate(
            [spectra[:, at : at + 16, :].reshape(256, LANES) for at in starts], axis=1
        )
        rows = apply(rows, coulombs)
        for part, at in enumerate(starts):
            out[:, at : at + 16, :] = rows[:, part * LANES : part * LANES + LANES].reshape(
                PEERS, 16, LANES
            )

    at = 32 * UNITS
    rows = spectra[:, at:, :]
    rows = jnp.concatenate([rows, pltpu.roll(rows, N, 2)], axis=1).reshape(256, LANES)
    mine = jnp.where(on_first(), first, second)
    rows = apply(rows, rows_of((mine, swap(mine)))).reshape(PEERS, 16, LANES)
    behind = pltpu.roll(rows[:, 8:], N, 2)
    front = lax.broadcasted_iota(jnp.int32, behind.shape, 2) < N
    out[:, at:, :] = jnp.where(front, rows[:, :8], behind)


def backward_kernel(
    returned,
    own_blocks,
    blocks,
    table_y_back,
    table_z_back,
    own_field,
    shared_field,
    lone_field,
    other_field,
    fields,
):
    started = set()

    def add(place, plane, value):
        if not isinstance(place, int) or (place, plane) in started:
            fields[4 * place + plane] += value
        else:
            started.add((place, plane))
            fields[4 * place + plane] = value

    read = reader(own_blocks, blocks)

    def collect(unit, half, plane, potential):
        left, right = places(unit)
        partner = turned(unit, half, read(right, plane))
        given = turned(unit, half, potential * read(left, plane))
        if unit == EIGHT and half:
            squares = jnp.where(on_eight(), potential, 0.0)
            potential = potential - squares
            given = jnp.where(on_eight(), 0.0, given)
            add(0, plane, squares * read(0, plane))
        add(left, plane, potential * partner)
        add(right, plane, given)

    def potentials(pairs, table_z_back):
        rows = table_times(table_y_back, jnp.concatenate(pairs, axis=1))
        planes_of = [
            jnp.concatenate(
                [
                    rows[
                        at * LANES + part * N : at * LANES + part * N + N,
                        high * LANES : high * LANES + LANES,
                    ]
                    for part in range(2)
                ],
                axis=1,
            )
            for high in range(len(pairs))
            for at in range(2)
        ]
        return times_table(jnp.concatenate(planes_of, axis=0), table_z_back)

    for u in range(UNITS):
        pairs = []
        for high in range(2):
            at = 32 * u + 8 * high
            both = [returned[:, at : at + 8, :], returned[:, at + 16 : at + 24, :]]
            pairs.append(jnp.concatenate(both, axis=1).reshape(256, LANES))
        rows = potentials(pairs, table_z_back)
        for plane in range(4):
            for half in range(2):
                collect(
                    u,
                    half,
                    plane,
                    rows[plane * N : plane * N + N, half * LANES : half * LANES + LANES],
                )
    last = returned[:, 32 * UNITS :, :]
    last = [jnp.where(on_first(), last, 0.0), jnp.where(on_first(), 0.0, last)]
    last = [jnp.concatenate(last, axis=1).reshape(256, LANES)]
    rows = potentials(last, table_z_back[:, :, :LANES])
    low = low_lanes(N)
    for at in range(2):
        potential = rows[at * N : at * N + N, :LANES]
        other = swap(potential)
        fields[at] += jnp.where(low, potential, other) * swap(own_blocks[at])
        fields[2 + at] += jnp.where(low, other, potential) * swap(own_blocks[2 + at])
    for place, field in enumerate((own_field, shared_field, lone_field, other_field)):
        field[...] = fields[4 * place : 4 * place + 4]


def share_kernel(mine, others, relayed, field):
    at = 4 * (1 - lax.axis_index("pool"))
    for plane in range(4):
        field[plane] = mine[plane] + others[at + plane] + relayed[plane]


def final_kernel(both, out):
    low = low_lanes(HALF)
    for plane in range(4):
        even, odd = (
            both[plane, at : at + HALF] + both[4 + plane, at : at + HALF] for at in (0, HALF)
        )
        out[pl.ds(plane, HALF, stride=4), :] = jnp.where(low, even, swap(odd))
        out[pl.ds(128 + plane, HALF, stride=4), :] = jnp.where(low, swap(even), odd)


VMEM = pl.BlockSpec(memory_space=pltpu.VMEM)
PARAMS = pltpu.CompilerParams(vmem_limit_bytes=32 * 1024 * 1024)
CHUNKS = jax.ShapeDtypeStruct((PEERS, ROWS, LANES), jnp.float32)


def planes(count):
    return jax.ShapeDtypeStruct((count, N, LANES), jnp.float32)


LONG = pl.CostEstimate(flops=10**10, bytes_accessed=10**6, transcendentals=0)


def first(own):
    return pl.pallas_call(
        first_kernel,
        out_shape=[planes(4), jax.ShapeDtypeStruct((256, LANES), jnp.float32)],
        in_specs=[VMEM],
        out_specs=[VMEM] * 2,
        compiler_params=PARAMS,
        cost_estimate=LONG,
    )(own)


def forward(own_blocks, shared, alone, table_z, table_y):
    return pl.pallas_call(
        forward_kernel,
        out_shape=[CHUNKS, planes(12)],
        in_specs=[VMEM] * 5,
        out_specs=[VMEM] * 2,
        compiler_params=PARAMS,
    )(own_blocks, shared, alone, table_z, table_y)


def middle(spectra, kernel, table_x, table_x_back):
    return pl.pallas_call(
        middle_kernel,
        out_shape=CHUNKS,
        in_specs=[VMEM] * 4,
        out_specs=VMEM,
        compiler_params=PARAMS,
    )(spectra, kernel, table_x, table_x_back)


def backward(returned, own_blocks, blocks, table_y_back, table_z_back):
    return pl.pallas_call(
        backward_kernel,
        out_shape=[planes(4)] * 4,
        in_specs=[VMEM] * 5,
        out_specs=[VMEM] * 4,
        scratch_shapes=[pltpu.VMEM((16, N, LANES), jnp.float32)],
        compiler_params=PARAMS,
    )(returned, own_blocks, blocks, table_y_back, table_z_back)


def share(mine, others, relayed):
    return pl.pallas_call(
        share_kernel,
        out_shape=planes(4),
        in_specs=[VMEM] * 3,
        out_specs=VMEM,
        compiler_params=PARAMS,
    )(mine, others, relayed)


def final(both):
    return pl.pallas_call(
        final_kernel,
        out_shape=jax.ShapeDtypeStruct((256, LANES), jnp.float32),
        in_specs=[VMEM],
        out_specs=VMEM,
        compiler_params=PARAMS,
    )(both)


def along_band(value, steps, crossed=False):
    count = lax.axis_size("band")
    pairs = [
        (2 * source + core, 2 * ((source + steps[core]) % count) + (core ^ crossed))
        for source in range(count)
        for core in range(2)
    ]
    return lax.ppermute(value, ("band", "pool"), pairs)


def both_cores(value):
    return lax.all_gather(value, "pool", tiled=True)


def exchange(value):
    return lax.all_to_all(value, "fft", split_axis=0, concat_axis=0, tiled=True)


def local(orbitals, kernel):
    table_z, table_y, table_x, table_x_back, table_y_back, table_z_back = [
        jnp.asarray(t) for t in tables()
    ]
    own = orbitals.reshape(2, 4, HALF, LANES).transpose(0, 2, 1, 3).reshape(256, LANES)
    shared = both_cores(along_band(own, [-s for s in SHARED]))
    own_blocks, own_again = first(own)
    alone = along_band(own_again, [-s for s in ALONE])
    spectra, blocks = forward(own_blocks, shared, alone, table_z, table_y)
    returned = exchange(middle(exchange(spectra), kernel, table_x, table_x_back))
    own_field, shared_field, lone_field, other_field = backward(
        returned, own_blocks, blocks, table_y_back, table_z_back
    )
    relayed = along_band(lone_field, RELAY, True)
    shared_field = along_band(share(shared_field, both_cores(other_field), relayed), SHARED)
    field = final(both_cores(shared_field + own_field))
    return field.reshape(2, HALF, 4, LANES).transpose(0, 2, 1, 3).reshape(2, 4, N * N)


def solution(mesh):
    return jax.shard_map(
        local,
        mesh=mesh,
        in_specs=(P("band", "fft", None), P(None, "fft")),
        out_specs=P("band", "fft", None),
        check_vma=False,
    )
```

```python
import jax
import jax.numpy as jnp
import ml_dtypes
import numpy as np
from jax import lax
from jax.experimental import pallas as pl
from jax.experimental.pallas import tpu as pltpu
from jax.sharding import PartitionSpec as P

N = 64
HALF = N // 2
CELLS = N * N * N
LANES = 2 * N
PEERS = 16
UNITS = 4
ROWS = 32 * UNITS + 8

SHARED = (-3, 4)
ALONE = (5, -2)
RELAY = (1, 1)
MEETINGS = (((0, 2), (0, 2)), ((0, 1), (0, 1)), ((1, 3), (2, 3)), ((1, 2), (1, 2)))
EIGHT = 3
EIGHT_CORE = 0


def wave_parts(rows, columns):
    angle = 2.0 * np.pi / N * ((rows * columns) % N)
    return np.cos(angle), np.sin(angle)


def split_table(table):
    high = table.astype(ml_dtypes.bfloat16)
    low = (table - high.astype(np.float64)).astype(ml_dtypes.bfloat16)
    return np.stack([high, low])


def tables():
    index = np.arange(N)
    cosine, sine = wave_parts(index[:, None], index[None, :])
    turn = np.stack([np.stack([cosine, sine]), np.stack([-sine, cosine])])
    two = np.eye(2)
    along_z = np.einsum("oikz,ab->iazobk", turn, two).reshape(256, 256)
    along_y = np.einsum("oiky,ab->kaoiby", turn, two)
    along_y = along_y.reshape(PEERS, 2, 2, 2, 2, 2, 2, HALF, 2)
    along_y = along_y.transpose(0, 1, 4, 3, 2, 6, 5, 8, 7).reshape(256, 256)
    along_x = np.einsum("oikx,ab->oakxib", turn, two).reshape(2, 2, N, HALF, 2, 2, 2)
    along_x = along_x.transpose(0, 1, 2, 3, 5, 4, 6).reshape(256, 256)
    return [split_table(t) for t in (along_z, along_y, along_x, along_x.T, along_y.T, along_z.T)]


def halves(value):
    high = value.astype(jnp.bfloat16)
    low = (value - high.astype(jnp.float32)).astype(jnp.bfloat16)
    return high, low


def dot(left, right):
    return jnp.dot(left, right, preferred_element_type=jnp.float32)


def times_table(value, table):
    high, low = halves(value)
    rows = value.shape[0]
    both = dot(jnp.concatenate([high, low], axis=0), table[0])
    return both[:rows] + both[rows:] + dot(high, table[1])


def table_times(table, value):
    high, low = halves(value)
    rows = table.shape[1]
    both = dot(jnp.concatenate([table[0], table[1]], axis=0), high)
    return both[:rows] + both[rows:] + dot(table[0], low)


def swap(value):
    return pltpu.roll(value, N, 1)


def low_lanes(rows):
    return lax.broadcasted_iota(jnp.int32, (rows, LANES), 1) < N


def on_first():
    return lax.axis_index("pool") == 0


def on_eight():
    return lax.axis_index("pool") == EIGHT_CORE


def pick(first, second):
    return first if first is second else jnp.where(on_first(), first, second)


def places(unit):
    first, second = MEETINGS[unit]
    return pick(first[0], second[0]), pick(first[1], second[1])


def turned(unit, half, value):
    if unit == EIGHT and not half:
        return jnp.where(on_eight() & (lax.axis_index("band") >= 8), swap(value), value)
    return swap(value) if half else value


def reader(own_blocks, blocks):
    def read(place, plane):
        if isinstance(place, int):
            return blocks[4 * place - 4 + plane] if place else own_blocks[plane]
        return blocks[4 * place - 4 + plane]

    return read


def unfold(source, base, blocks, place):
    low = low_lanes(HALF)
    for plane in range(4):
        first = source[pl.ds(base + plane, HALF, stride=4), :]
        second = source[pl.ds(base + 128 + plane, HALF, stride=4), :]
        blocks[4 * place + plane, :HALF] = jnp.where(low, first, swap(second))
        blocks[4 * place + plane, HALF:] = jnp.where(low, swap(first), second)


def first_kernel(own, blocks, again):
    unfold(own, 0, blocks, 0)
    again[...] = own[...]


def spectrum(density, table_z, table_y):
    rows = times_table(jnp.concatenate(density, axis=0), table_z)
    pairs = [
        jnp.concatenate(
            [
                rows[base + at * N : base + at * N + N, part * LANES : part * LANES + LANES]
                for at in range(2)
                for part in range(2)
            ],
            axis=0,
        )
        for base in range(0, rows.shape[0], LANES)
    ]
    rows = jnp.concatenate(pairs, axis=1)
    return table_times(table_y, rows).reshape(PEERS, 16, rows.shape[1])


def forward_kernel(own_blocks, shared, alone, table_z, table_y, out, blocks):
    core = lax.axis_index("pool")
    unfold(shared, 256 * core, blocks, 0)
    unfold(alone, 0, blocks, 1)
    unfold(shared, 256 * (1 - core), blocks, 2)
    read = reader(own_blocks, blocks)

    def density(unit, half, plane):
        left, right = places(unit)
        left, right = read(left, plane), turned(unit, half, read(right, plane))
        if unit == EIGHT and half:
            own = read(0, plane)
            left, right = jnp.where(on_eight(), own, left), jnp.where(on_eight(), own, right)
        return left * right

    for u in range(UNITS):
        rows = spectrum(
            [
                jnp.concatenate([density(u, 0, plane), density(u, 1, plane)], axis=1)
                for plane in range(4)
            ],
            table_z,
            table_y,
        )
        for ky_high in range(2):
            for high in range(2):
                at = 32 * u + 16 * ky_high + 8 * high
                out[:, at : at + 8, :] = rows[
                    :, 8 * ky_high : 8 * ky_high + 8, LANES * high : LANES * high + LANES
                ]

    last = []
    for at, behind in ((own_blocks[0], own_blocks[2]), (own_blocks[1], own_blocks[3])):
        pairs = jnp.where(low_lanes(N), at * swap(at), behind * swap(behind))
        last.append(pairs)
    rows = spectrum(last, table_z[:, :LANES], table_y)
    out[:, 32 * UNITS :, :] = jnp.where(on_first(), rows[:, :8], rows[:, 8:])


def middle_kernel(spectra, kernel, table_x, table_x_back, out):
    low = low_lanes(N)
    first, second = (kernel[:, at : at + LANES] * (-1.0 / CELLS) for at in (0, LANES))

    def twice(value):
        other = swap(value)
        return jnp.where(low, value, other), jnp.where(low, other, value)

    def rows_of(pair):
        return jnp.concatenate([*pair, *pair], axis=0)

    def apply(rows, coulomb):
        return table_times(table_x_back, table_times(table_x, rows) * coulomb)

    coulombs = jnp.concatenate([rows_of(twice(first)), rows_of(twice(second))], axis=1)
    for u in range(UNITS):
        starts = 32 * u, 32 * u + 16
        rows = jnp.concatenate(
            [spectra[:, at : at + 16, :].reshape(256, LANES) for at in starts], axis=1
        )
        rows = apply(rows, coulombs)
        for part, at in enumerate(starts):
            out[:, at : at + 16, :] = rows[:, part * LANES : part * LANES + LANES].reshape(
                PEERS, 16, LANES
            )

    at = 32 * UNITS
    rows = spectra[:, at:, :]
    rows = jnp.concatenate([rows, pltpu.roll(rows, N, 2)], axis=1).reshape(256, LANES)
    mine = jnp.where(on_first(), first, second)
    rows = apply(rows, rows_of((mine, swap(mine)))).reshape(PEERS, 16, LANES)
    behind = pltpu.roll(rows[:, 8:], N, 2)
    front = lax.broadcasted_iota(jnp.int32, behind.shape, 2) < N
    out[:, at:, :] = jnp.where(front, rows[:, :8], behind)


def backward_kernel(
    returned,
    own_blocks,
    blocks,
    table_y_back,
    table_z_back,
    own_field,
    shared_field,
    lone_field,
    other_field,
    fields,
):
    started = set()

    def add(place, plane, value):
        if not isinstance(place, int) or (place, plane) in started:
            fields[4 * place + plane] += value
        else:
            started.add((place, plane))
            fields[4 * place + plane] = value

    read = reader(own_blocks, blocks)

    def collect(unit, half, plane, potential):
        left, right = places(unit)
        partner = turned(unit, half, read(right, plane))
        given = turned(unit, half, potential * read(left, plane))
        if unit == EIGHT and half:
            squares = jnp.where(on_eight(), potential, 0.0)
            potential = potential - squares
            given = jnp.where(on_eight(), 0.0, given)
            add(0, plane, squares * read(0, plane))
        add(left, plane, potential * partner)
        add(right, plane, given)

    def potentials(pairs, table_z_back):
        rows = table_times(table_y_back, jnp.concatenate(pairs, axis=1))
        planes_of = [
            jnp.concatenate(
                [
                    rows[
                        at * LANES + part * N : at * LANES + part * N + N,
                        high * LANES : high * LANES + LANES,
                    ]
                    for part in range(2)
                ],
                axis=1,
            )
            for high in range(len(pairs))
            for at in range(2)
        ]
        return times_table(jnp.concatenate(planes_of, axis=0), table_z_back)

    for u in range(UNITS):
        pairs = []
        for high in range(2):
            at = 32 * u + 8 * high
            both = [returned[:, at : at + 8, :], returned[:, at + 16 : at + 24, :]]
            pairs.append(jnp.concatenate(both, axis=1).reshape(256, LANES))
        rows = potentials(pairs, table_z_back)
        for plane in range(4):
            for half in range(2):
                collect(
                    u,
                    half,
                    plane,
                    rows[plane * N : plane * N + N, half * LANES : half * LANES + LANES],
                )
    last = returned[:, 32 * UNITS :, :]
    last = [jnp.where(on_first(), last, 0.0), jnp.where(on_first(), 0.0, last)]
    last = [jnp.concatenate(last, axis=1).reshape(256, LANES)]
    rows = potentials(last, table_z_back[:, :, :LANES])
    low = low_lanes(N)
    for at in range(2):
        potential = rows[at * N : at * N + N, :LANES]
        other = swap(potential)
        fields[at] += jnp.where(low, potential, other) * swap(own_blocks[at])
        fields[2 + at] += jnp.where(low, other, potential) * swap(own_blocks[2 + at])
    for place, field in enumerate((own_field, shared_field, lone_field, other_field)):
        field[...] = fields[4 * place : 4 * place + 4]


def share_kernel(mine, others, relayed, field):
    at = 4 * (1 - lax.axis_index("pool"))
    for plane in range(4):
        field[plane] = mine[plane] + others[at + plane] + relayed[plane]


def final_kernel(both, out):
    low = low_lanes(HALF)
    for plane in range(4):
        even, odd = (
            both[plane, at : at + HALF] + both[4 + plane, at : at + HALF] for at in (0, HALF)
        )
        out[pl.ds(plane, HALF, stride=4), :] = jnp.where(low, even, swap(odd))
        out[pl.ds(128 + plane, HALF, stride=4), :] = jnp.where(low, swap(even), odd)


VMEM = pl.BlockSpec(memory_space=pltpu.VMEM)
PARAMS = pltpu.CompilerParams(vmem_limit_bytes=32 * 1024 * 1024)
CHUNKS = jax.ShapeDtypeStruct((PEERS, ROWS, LANES), jnp.float32)


def planes(count):
    return jax.ShapeDtypeStruct((count, N, LANES), jnp.float32)


LONG = pl.CostEstimate(flops=10**10, bytes_accessed=10**6, transcendentals=0)


def first(own):
    return pl.pallas_call(
        first_kernel,
        out_shape=[planes(4), jax.ShapeDtypeStruct((256, LANES), jnp.float32)],
        in_specs=[VMEM],
        out_specs=[VMEM] * 2,
        compiler_params=PARAMS,
        cost_estimate=LONG,
    )(own)


def forward(own_blocks, shared, alone, table_z, table_y):
    return pl.pallas_call(
        forward_kernel,
        out_shape=[CHUNKS, planes(12)],
        in_specs=[VMEM] * 5,
        out_specs=[VMEM] * 2,
        compiler_params=PARAMS,
    )(own_blocks, shared, alone, table_z, table_y)


def middle(spectra, kernel, table_x, table_x_back):
    return pl.pallas_call(
        middle_kernel,
        out_shape=CHUNKS,
        in_specs=[VMEM] * 4,
        out_specs=VMEM,
        compiler_params=PARAMS,
    )(spectra, kernel, table_x, table_x_back)


def backward(returned, own_blocks, blocks, table_y_back, table_z_back):
    return pl.pallas_call(
        backward_kernel,
        out_shape=[planes(4)] * 4,
        in_specs=[VMEM] * 5,
        out_specs=[VMEM] * 4,
        scratch_shapes=[pltpu.VMEM((16, N, LANES), jnp.float32)],
        compiler_params=PARAMS,
    )(returned, own_blocks, blocks, table_y_back, table_z_back)


def share(mine, others, relayed):
    return pl.pallas_call(
        share_kernel,
        out_shape=planes(4),
        in_specs=[VMEM] * 3,
        out_specs=VMEM,
        compiler_params=PARAMS,
    )(mine, others, relayed)


def final(both):
    return pl.pallas_call(
        final_kernel,
        out_shape=jax.ShapeDtypeStruct((256, LANES), jnp.float32),
        in_specs=[VMEM],
        out_specs=VMEM,
        compiler_params=PARAMS,
    )(both)


def along_band(value, steps, crossed=False):
    count = lax.axis_size("band")
    pairs = [
        (2 * source + core, 2 * ((source + steps[core]) % count) + (core ^ crossed))
        for source in range(count)
        for core in range(2)
    ]
    return lax.ppermute(value, ("band", "pool"), pairs)


def both_cores(value):
    return lax.all_gather(value, "pool", tiled=True)


def exchange(value):
    return lax.all_to_all(value, "fft", split_axis=0, concat_axis=0, tiled=True)


def local(orbitals, kernel):
    table_z, table_y, table_x, table_x_back, table_y_back, table_z_back = [
        jnp.asarray(t) for t in tables()
    ]
    own = orbitals.reshape(2, 4, HALF, LANES).transpose(0, 2, 1, 3).reshape(256, LANES)
    shared = both_cores(along_band(own, [-s for s in SHARED]))
    own_blocks, own_again = first(own)
    alone = along_band(own_again, [-s for s in ALONE])
    spectra, blocks = forward(own_blocks, shared, alone, table_z, table_y)
    returned = exchange(middle(exchange(spectra), kernel, table_x, table_x_back))
    own_field, shared_field, lone_field, other_field = backward(
        returned, own_blocks, blocks, table_y_back, table_z_back
    )
    relayed = along_band(lone_field, RELAY, True)
    shared_field = along_band(share(shared_field, both_cores(other_field), relayed), SHARED)
    field = final(both_cores(shared_field + own_field))
    return field.reshape(2, HALF, 4, LANES).transpose(0, 2, 1, 3).reshape(2, 4, N * N)


def solution(mesh):
    return jax.shard_map(
        local,
        mesh=mesh,
        in_specs=(P("band", "fft", None), P(None, "fft")),
        out_specs=P("band", "fft", None),
        check_vma=False,
    )
```
